256 devices in a mesh: tm: 64 (over x_hi, y, z), chan: 4 (over x_lo, core).
Axes of the slice: x: 4 (x_hi: 2, x_lo: 2; x = x_hi * 2 + x_lo), y: 4, z: 8, core: 2. Of those that a mesh axis runs over, the one named last changes fastest.
Arguments:
- tokens: bfloat16 [131072, 1024], P('tm', 'chan'), may hold values from -170 to 170
- w_query: bfloat16 [1024, 1024], P(None, 'chan'), may hold values from -0.1875 to 0.1875
- w_key: bfloat16 [1024, 1024], P(None, 'chan'), may hold values from -0.1875 to 0.1875
- w_value: bfloat16 [1024, 1024], P(None, 'chan'), may hold values from -0.1875 to 0.1875
- w_out: bfloat16 [1024, 1024], P('chan'), may hold values from -0.25 to 0.25
- pool_kernel: float32 [2, 27, 64], replicated, may hold values from -1.25 to 1.25
Outputs:
- block_out: bfloat16 [131072, 1024], P('tm', 'chan')
The draws below stay inside these ranges and needn't reach their ends.
All inputs are finite; a program needn't handle non-finite values.
Results may differ from the reference program's by a relative error of at most 0.0053.
Values may be sent and summed in bfloat16 or wider, within the bound.
No kernel may reach another device: no remote copies, remote signals or barrier semaphores. Data moves between devices by JAX's collectives and lax.ppermute only.
A program may use at most 128 MiB of HBM per device.

```python
import math
import jax
import jax.numpy as jnp
from jax import lax

D = 1024
HEADS = 16
HDIM = 64
HH = 16
WW = 16
TOK_DEV = 2048
POOLED = 64
FRAMES = 512
TOKENS = 131072
N_TM = 64


def draw_tokens(key, part):
    first_key = jax.random.fold_in(key, 0)
    normal_draw = jax.random.normal(first_key, (TOKENS, D), jnp.float32)
    return jnp.clip(normal_draw, -6.0, 6.0).astype(jnp.bfloat16)


def spiked(values, key, source, target, parts, factor):
    def block_of(position):
        return (jnp.arange(values.shape[position]) // (values.shape[position] // parts)).reshape((-1,) + (1,) * (values.ndim - 1 - position))

    first = jax.random.permutation(key, parts)[block_of(target)]
    second = (block_of(target) + parts // 2) % parts
    return jnp.where((block_of(source) == first) | (block_of(source) == second), factor * values, values)


def shard_levels(rng, shape, pieces, smallest, high):
    level, own = 1.0, jax.random.fold_in(rng, 6)
    for position, blocks in pieces:
        heights = jnp.exp(jax.random.uniform(jax.random.fold_in(own, position), (blocks,), jnp.float32, smallest / len(pieces), high / len(pieces)))
        level = level * jnp.repeat(heights, shape[position] // blocks).reshape([-1 if axis == position else 1 for axis in range(len(shape))])
    return level


def bell_draw(stream_key, shape, deviation, bound, shards=(), kind=jnp.bfloat16):
    result = jax.random.normal(stream_key, shape, jnp.float32) * deviation
    if len(shards) > 0:
        result = shard_levels(stream_key, shape, shards, -0.22, 0.18) * result
    return jnp.clip(result, min=-bound, max=bound).astype(kind)


def noise_with(key, extent, scale, most, shards, heavy, held_as=jnp.bfloat16):
    drawn = scale * jax.random.normal(key, extent, jnp.float32)
    if shards:
        drawn = drawn * shard_levels(key, extent, shards, -0.22, 0.18)
    return jnp.clip(spiked(drawn, jax.random.fold_in(key, 3), *heavy), -most, most).astype(held_as)


def setup_inputs(seed: int = 0) -> dict:
    key_of = jax.random.split(jax.random.key(seed), 7)
    return {
        "tokens": draw_tokens(jax.random.fold_in(key_of[6], 71), 0),
        "w_query": bell_draw(key_of[1], (D, D), D ** -0.5, 0.1875, ((1, 4),)),
        "w_key": bell_draw(key_of[2], (D, D), D ** -0.5, 0.1875, ((1, 4),)),
        "w_value": bell_draw(key_of[3], (D, D), D ** -0.5, 0.1875, ((1, 4),)),
        "w_out": noise_with(key_of[4], (D, D), D ** -0.5, 0.25, ((0, 4),), (0, 1, 4, 2.0)),
        "pool_kernel": bell_draw(key_of[5], (2, 27, HDIM), 27 ** -0.5, 1.25, (), jnp.float32),
    }


epsilon = 1e-06

def head_norm(field, head_width):
    shape = field.shape
    split = field.reshape(shape[:-1] + (shape[-1] // head_width, head_width))
    center = split - lax.optimization_barrier(jnp.mean(split, axis=-1, keepdims=True))
    spread = lax.optimization_barrier(jnp.mean(center * center, axis=-1, keepdims=True))
    return (center * lax.rsqrt(spread + epsilon)).reshape(shape)

def pool_field(field, kernel):
    earlier = jnp.roll(field, 1, axis=0)
    sources = (earlier[0::2], field[0::2], field[1::2])
    running = jnp.zeros((field.shape[0] // 2, HH // 4, WW // 4, field.shape[3]), jnp.float32)
    for first in range(3):
        padded = jnp.pad(sources[first], ((0, 0), (1, 0), (1, 0), (0, 0)))
        for second in range(3):
            for third in range(3):
                picked = padded[:, second:second + HH:4, third:third + WW:4, :]
                running = running + picked * kernel[9 * first + 3 * second + third]
    return running

def reference(tokens, w_query, w_key, w_value, w_out, pool_kernel):
    reach = min(6, (N_TM - 1) // 2)
    key_all = jnp.dot(tokens, w_key, preferred_element_type=jnp.float32).astype(jnp.bfloat16)
    value_all = jnp.dot(tokens, w_value, preferred_element_type=jnp.float32).astype(jnp.bfloat16)
    kernel_k = jnp.tile(pool_kernel[0], (1, HEADS))
    kernel_v = jnp.tile(pool_kernel[1], (1, HEADS))
    pooled_k = pool_field(key_all.astype(jnp.float32).reshape(FRAMES, HH, WW, D), kernel_k)
    pooled_k = head_norm(pooled_k, HDIM).astype(jnp.bfloat16).reshape(N_TM, POOLED, D)
    pooled_v = pool_field(value_all.astype(jnp.float32).reshape(FRAMES, HH, WW, D), kernel_v)
    pooled_v = head_norm(pooled_v, HDIM).astype(jnp.bfloat16).reshape(N_TM, POOLED, D)

    def one_block(index):
        rows_here = lax.dynamic_slice_in_dim(tokens, (index * TOK_DEV).astype(jnp.int32), TOK_DEV, 0)
        queries = jnp.dot(rows_here, w_query, preferred_element_type=jnp.float32).astype(jnp.bfloat16)
        chosen = (index + jnp.arange(-reach, reach + 1, dtype=jnp.int32)) % N_TM
        key_rows = pooled_k[chosen].reshape(-1, HEADS, HDIM).astype(jnp.float32)
        value_rows = pooled_v[chosen].reshape(-1, HEADS, HDIM).astype(jnp.float32)
        query_heads = queries.astype(jnp.float32).reshape(TOK_DEV, HEADS, HDIM)
        scores = jnp.einsum('qhd,khd->hqk', query_heads, key_rows) / math.sqrt(HDIM)
        highest = lax.optimization_barrier(jnp.max(scores, axis=-1, keepdims=True))
        weighted = jnp.exp(scores - highest)
        summed = lax.optimization_barrier(jnp.sum(weighted, axis=-1))
        weights_bf = weighted.astype(jnp.bfloat16).astype(jnp.float32)
        blended = jnp.einsum('hqk,khd->qhd', weights_bf, value_rows)
        attended = (blended / summed.T[:, :, None] + query_heads).astype(jnp.bfloat16).reshape(TOK_DEV, D)
        projected = jnp.dot(attended, w_out, preferred_element_type=jnp.float32)
        return (rows_here.astype(jnp.float32) + projected).astype(jnp.bfloat16)
    return lax.map(one_block, jnp.arange(N_TM, dtype=jnp.int32)).reshape(TOKENS, D)
```

```python
import functools
import math

import jax
import jax.numpy as jnp
import ml_dtypes
import numpy as np
from jax import lax
from jax.experimental import pallas as pl
from jax.experimental.pallas import tpu as pltpu
from jax.sharding import PartitionSpec as P

D = 1024
HDIM = 64
HH = 16
WW = 16
FRAME = HH * WW
POOL_ROWS = (HH // 4) * (WW // 4)
TAP_ROWS = 9 * POOL_ROWS
REST_ROWS = FRAME - TAP_ROWS
RING = 8
REACH = 6
CHUNKS = 4
EPSILON = 1e-06
MB = 1024 * 1024


def tap_order():
    order = []
    used = set()
    for second in range(3):
        for third in range(3):
            for row in range(HH // 4):
                for col in range(WW // 4):
                    i, j = 4 * row - 1 + second, 4 * col - 1 + third
                    inside = i >= 0 and j >= 0
                    order.append(i * WW + j if inside else None)
                    if inside:
                        used.add(i * WW + j)
    others = [t for t in range(FRAME) if t not in used]
    order = [others.pop(0) if t is None else t for t in order]
    return np.array(order + others)


ORDER = tap_order()
GATHER = (ORDER[:, None] == np.arange(FRAME)[None, :]).astype(ml_dtypes.bfloat16)


def vmem(count):
    return [pl.BlockSpec(memory_space=pltpu.VMEM)] * count


def params(limit=48):
    return pltpu.CompilerParams(vmem_limit_bytes=limit * MB)


def cost(flops, moved, exps=0):
    return pl.CostEstimate(flops=int(flops), bytes_accessed=int(moved), transcendentals=int(exps))


def dot(a, b):
    return jnp.dot(a, b, preferred_element_type=jnp.float32)


def arrange_kernel(gather_ref, tokens_ref, taps_ref, last_ref, rest_ref):
    frames = tokens_ref.shape[0] // FRAME
    for f in range(frames):
        moved = dot(gather_ref[...], tokens_ref[f * FRAME : (f + 1) * FRAME, :]).astype(jnp.bfloat16)
        if f < frames - 1:
            taps_ref[f * TAP_ROWS : (f + 1) * TAP_ROWS, :] = moved[:TAP_ROWS]
        else:
            last_ref[...] = moved[:TAP_ROWS]
        rest_ref[f * REST_ROWS : (f + 1) * REST_ROWS, :] = moved[TAP_ROWS:]


def weight_rows(ref, me, k):
    width = ref.shape[0] // 4
    return ref[pl.ds(pl.multiple_of((me ^ k) * width, width), width), :]


def project(pieces, start, count, weights):
    total = dot(pieces[0][start : start + count, :], weights[0])
    for k in range(1, 4):
        total = total + dot(pieces[k][start : start + count, :], weights[k])
    return total


def tap_masks(width):
    row = lax.broadcasted_iota(jnp.int32, (POOL_ROWS, width), 0)
    top = row >= WW // 4
    left = (row % (WW // 4)) > 0
    return top, left


def weigh(slabs, taps, first, masks):
    top, left = masks
    total = None
    for second in range(3):
        for third in range(3):
            q = 3 * second + third
            slab = slabs[q * POOL_ROWS : (q + 1) * POOL_ROWS]
            if second == 0:
                slab = jnp.where(top, slab, 0.0)
            if third == 0:
                slab = jnp.where(left, slab, 0.0)
            term = slab * taps[9 * first + q : 9 * first + q + 1, :]
            total = term if total is None else total + term
    return total


def halo_kernel(p0, p1, p2, p3, wk_ref, wv_ref, taps_ref, halo_ref):
    me = lax.axis_index("chan")
    width = wk_ref.shape[1]
    masks = tap_masks(width)
    for side, w_ref in enumerate((wk_ref, wv_ref)):
        weights = [weight_rows(w_ref, me, k) for k in range(4)]
        lanes = slice(side * width, (side + 1) * width)
        rows = project((p0, p1, p2, p3), 0, TAP_ROWS, weights)
        rows = rows.astype(jnp.bfloat16).astype(jnp.float32)
        halo_ref[:, lanes] = weigh(rows, taps_ref[:, lanes], 0, masks)


def group_mean(rows, averaging):
    high = rows.astype(jnp.bfloat16)
    rest = rows - high.astype(jnp.float32)
    middle = rest.astype(jnp.bfloat16)
    low = (rest - middle.astype(jnp.float32)).astype(jnp.bfloat16)
    return dot(high, averaging) + dot(middle, averaging) + dot(low, averaging)


def pool_kernel_body(a0, a1, a2, a3, l0, l1, l2, l3, wk_ref, wv_ref, taps_ref, halo_ref, out_ref):
    me = lax.axis_index("chan")
    width = wk_ref.shape[1]
    masks = tap_masks(width)
    lane = lax.broadcasted_iota(jnp.int32, (width, width), 1) // HDIM
    row = lax.broadcasted_iota(jnp.int32, (width, width), 0) // HDIM
    averaging = jnp.where(lane == row, 1.0 / HDIM, 0.0).astype(jnp.bfloat16)
    pooled_frames = out_ref.shape[0] // POOL_ROWS
    frames = 2 * pooled_frames
    for side, w_ref in enumerate((wk_ref, wv_ref)):
        weights = [weight_rows(w_ref, me, k) for k in range(4)]
        lanes = slice(side * width, (side + 1) * width)
        taps = taps_ref[:, lanes]
        sums = [None] * pooled_frames
        sums[0] = halo_ref[:, lanes]
        for f in range(frames):
            if f < frames - 1:
                rows = project((a0, a1, a2, a3), f * TAP_ROWS, TAP_ROWS, weights)
            else:
                rows = project((l0, l1, l2, l3), 0, TAP_ROWS, weights)
            rows = rows.astype(jnp.bfloat16).astype(jnp.float32)
            t = f // 2
            part = weigh(rows, taps, 1 + f % 2, masks)
            sums[t] = part if sums[t] is None else sums[t] + part
            if f % 2 == 1 and t + 1 < pooled_frames:
                sums[t + 1] = weigh(rows, taps, 0, masks)
        for t in range(pooled_frames):
            center = sums[t] - group_mean(sums[t], averaging)
            spread = group_mean(center * center, averaging)
            out_ref[t * POOL_ROWS : (t + 1) * POOL_ROWS, lanes] = (center * lax.rsqrt(spread + EPSILON)).astype(
                jnp.bfloat16
            )


def query_kernel(a0, a1, a2, a3, l0, l1, l2, l3, b0, b1, b2, b3, wq_ref, back_ref, q_ref, both):
    me = lax.axis_index("chan")
    weights = [weight_rows(wq_ref, me, k) for k in range(4)]
    frames = q_ref.shape[0] // FRAME
    for f in range(frames):
        if f < frames - 1:
            first = project((a0, a1, a2, a3), f * TAP_ROWS, TAP_ROWS, weights)
        else:
            first = project((l0, l1, l2, l3), 0, TAP_ROWS, weights)
        both[f % 2, :TAP_ROWS, :] = first.astype(jnp.bfloat16)
        both[f % 2, TAP_ROWS:, :] = project((b0, b1, b2, b3), f * REST_ROWS, REST_ROWS, weights).astype(jnp.bfloat16)
        q_ref[f * FRAME : (f + 1) * FRAME, :] = dot(back_ref[...], both[f % 2]).astype(jnp.bfloat16)


def row_kernel(own, b1, b2, b3, b4, b5, b6, b7, out_ref):
    z = lax.rem(lax.axis_index("tm"), RING)
    block = own.shape[0]
    for d, ref in enumerate((own, b1, b2, b3, b4, b5, b6, b7)):
        place = lax.rem(z + d, RING)
        out_ref[pl.ds(pl.multiple_of(place * block, block), block), :] = ref[...]


def attend_kernel(q_ref, before_ref, here_ref, after_ref, out_ref, window, keys, values):
    width = q_ref.shape[1]
    heads = width // HDIM
    block = here_ref.shape[0] // RING
    count = keys.shape[1]
    z = lax.rem(lax.axis_index("tm"), RING)

    @pl.when(pl.program_id(0) == 0)
    def _():
        n = before_ref.shape[0]
        m = here_ref.shape[0]
        window[:n, :] = before_ref[...]
        window[n : n + m, :] = here_ref[...]
        window[n + m :, :] = after_ref[...]
        rows = window[pl.ds(pl.multiple_of(z * block, block), count), :]
        head = lax.broadcasted_iota(jnp.int32, (count, width), 1) // HDIM
        k = rows[:, :width].astype(jnp.float32) * (1.0 / math.sqrt(HDIM))
        v = rows[:, width:].astype(jnp.float32)
        for h in range(heads):
            keys[h] = jnp.where(head == h, k, 0.0).astype(jnp.bfloat16)
            values[h] = jnp.where(head == h, v, 0.0).astype(jnp.bfloat16)

    q = q_ref[...]
    total = q.astype(jnp.float32)
    for h in range(heads):
        scores = lax.dot_general(q, keys[h], (((1,), (1,)), ((), ())), preferred_element_type=jnp.float32)
        top = jnp.max(scores, axis=-1, keepdims=True)
        weighted = jnp.exp(scores - top)
        summed = jnp.sum(weighted, axis=-1, keepdims=True)
        total = total + dot(weighted.astype(jnp.bfloat16), values[h]) * (1.0 / summed)
    out_ref[...] = total.astype(jnp.bfloat16)


def out_kernel(a0, a1, a2, a3, w0, w1, w2, w3, tokens_ref, *rest):
    out_ref = rest[-1]
    total = tokens_ref[...].astype(jnp.float32)
    acc = dot(a0[...], w0[...])
    for a, w in ((a1, w1), (a2, w2), (a3, w3)):
        acc = acc + dot(a[...], w[...])
    out_ref[...] = (total + acc).astype(jnp.bfloat16)


def swap(array, k):
    return lax.ppermute(array, "chan", [(i, i ^ k) for i in range(4)])


def ring_fetch(array, d, devices):
    return lax.ppermute(
        array, "tm", [(RING * (i // RING) + (i + d) % RING, i) for i in range(devices)]
    )


def per_device(tokens, w_query, w_key, w_value, w_out, pool_kernel):
    rows, width = tokens.shape
    frames = rows // FRAME
    devices = lax.axis_size("tm")
    bf16 = jnp.bfloat16
    gather = jnp.asarray(GATHER)
    back = jnp.asarray(np.ascontiguousarray(GATHER.T))
    taps = jnp.concatenate(
        [jnp.tile(pool_kernel[0], (1, width // HDIM)), jnp.tile(pool_kernel[1], (1, width // HDIM))], axis=1
    )

    body, last, rest = pl.pallas_call(
        arrange_kernel,
        out_shape=(
            jax.ShapeDtypeStruct(((frames - 1) * TAP_ROWS, width), bf16),
            jax.ShapeDtypeStruct((TAP_ROWS, width), bf16),
            jax.ShapeDtypeStruct((frames * REST_ROWS, width), bf16),
        ),
        in_specs=vmem(2),
        out_specs=tuple(vmem(3)),
        compiler_params=params(),
        cost_estimate=cost(2 * rows * FRAME * width, 4 * rows * width),
        name="arrange",
    )(gather, tokens)

    def spread(piece):
        across = swap(piece, 2)
        beside = swap(piece, 1)
        return piece, beside, across, swap(across, 1)

    last_pieces = spread(last)
    body_pieces = spread(body)
    halo = pl.pallas_call(
        halo_kernel,
        out_shape=jax.ShapeDtypeStruct((POOL_ROWS, 2 * width), jnp.float32),
        in_specs=vmem(7),
        out_specs=vmem(1)[0],
        compiler_params=params(),
        cost_estimate=cost(2 * TAP_ROWS * D * 2 * width, 2 * D * 2 * width),
        name="halo",
    )(*last_pieces, w_key, w_value, taps)
    halo = lax.ppermute(halo, "tm", [(i, (i + 1) % devices) for i in range(devices)])
    rest_pieces = spread(rest)
    block = pl.pallas_call(
        pool_kernel_body,
        out_shape=jax.ShapeDtypeStruct((frames // 2 * POOL_ROWS, 2 * width), bf16),
        in_specs=vmem(12),
        out_specs=vmem(1)[0],
        compiler_params=params(),
        cost_estimate=cost(2 * frames * TAP_ROWS * D * 2 * width, 8 * rows * width),
        name="pool",
    )(*body_pieces, *last_pieces, w_key, w_value, taps, halo)

    fetched = [ring_fetch(block, d, devices) for d in (1, 7, 2, 6, 3, 5, 4)]
    by_place = dict(zip((1, 7, 2, 6, 3, 5, 4), fetched))
    ring = pl.pallas_call(
        row_kernel,
        out_shape=jax.ShapeDtypeStruct((RING * block.shape[0], 2 * width), bf16),
        in_specs=vmem(8),
        out_specs=vmem(1)[0],
        compiler_params=params(),
        cost_estimate=cost(0, 2 * RING * 2 * block.size),
        name="ring",
    )(block, *[by_place[d] for d in range(1, 8)])
    edge = (RING - 2) * block.shape[0]
    before = lax.ppermute(ring[-edge:], "tm", [(i, (i + RING) % devices) for i in range(devices)])
    after = lax.ppermute(ring[:edge], "tm", [((i + RING) % devices, i) for i in range(devices)])

    queries = pl.pallas_call(
        query_kernel,
        out_shape=jax.ShapeDtypeStruct((rows, width), bf16),
        in_specs=vmem(14),
        out_specs=vmem(1)[0],
        scratch_shapes=[pltpu.VMEM((2, FRAME, width), bf16)],
        compiler_params=params(),
        cost_estimate=cost(2 * rows * D * width, 10 * rows * width),
        name="query",
    )(*body_pieces, *last_pieces, *rest_pieces, w_query, back)

    chan = lax.axis_index("chan")
    w_out_later, block_later = lax.optimization_barrier((w_out, block))
    w_pieces = []
    for k in range(4):
        part = lax.dynamic_slice(w_out_later, (0, (chan ^ k) * width), (width, width))
        w_pieces.append(part if k == 0 else swap(part, k))

    count = (2 * REACH + 1) * block.shape[0]
    heads = width // HDIM
    chunk = rows // CHUNKS
    tile = 256
    steps = chunk // tile
    result = None
    for i in range(CHUNKS):
        attended = pl.pallas_call(
            attend_kernel,
            grid=(steps,),
            out_shape=jax.ShapeDtypeStruct((chunk, width), bf16),
            in_specs=[pl.BlockSpec((tile, width), lambda s, i=i: (i * steps + s, 0))] + vmem(3),
            out_specs=pl.BlockSpec((tile, width), lambda s: (s, 0)),
            scratch_shapes=[
                pltpu.VMEM((2 * edge + ring.shape[0], 2 * width), bf16),
                pltpu.VMEM((heads, count, width), bf16),
                pltpu.VMEM((heads, count, width), bf16),
            ],
            compiler_params=params(),
            cost_estimate=cost(4 * chunk * count * heads * width, 4 * chunk * width, chunk * count * heads),
            name=f"attend{i}",
        )(queries, before, ring, after)
        pieces = spread(attended)
        extra = () if result is None else (result,)
        result = pl.pallas_call(
            out_kernel,
            grid=(1,),
            out_shape=jax.ShapeDtypeStruct((rows, width), bf16),
            in_specs=[pl.BlockSpec((chunk, width), lambda s: (0, 0))] * 4
            + [pl.BlockSpec((width, width), lambda s: (0, 0))] * 4
            + [pl.BlockSpec((chunk, width), lambda s, i=i: (i, 0))]
            + [pl.BlockSpec(memory_space=pl.ANY)] * len(extra),
            out_specs=pl.BlockSpec((chunk, width), lambda s, i=i: (i, 0)),
            input_output_aliases={9: 0} if extra else {},
            compiler_params=params(),
            cost_estimate=cost(2 * chunk * D * width, 12 * chunk * width),
            name=f"out{i}",
        )(*pieces, *w_pieces, tokens, *extra)
    return result


def solution(mesh):
    return jax.shard_map(
        per_device,
        mesh=mesh,
        in_specs=(
            P("tm", "chan"),
            P(None, "chan"),
            P(None, "chan"),
            P(None, "chan"),
            P("chan", None),
            P(),
        ),
        out_specs=P("tm", "chan"),
        check_vma=False,
    )
```

```python
import functools
import math

import jax
import jax.numpy as jnp
import ml_dtypes
import numpy as np
from jax import lax
from jax.experimental import pallas as pl
from jax.experimental.pallas import tpu as pltpu
from jax.sharding import PartitionSpec as P

D = 1024
HDIM = 64
HH = 16
WW = 16
FRAME = HH * WW
POOL_ROWS = (HH // 4) * (WW // 4)
TAP_ROWS = FRAME // 2
RING = 8
REACH = 6
TILE = 256
CHUNKS = (1, 2, 2, 2, 1)
EPSILON = 1e-06
MB = 1024 * 1024


def tap_order():
    wanted = []
    for second in range(3):
        for third in range(3):
            for row in range(HH // 4):
                for col in range(WW // 4):
                    i, j = 4 * row - 1 + second, 4 * col - 1 + third
                    wanted.append(i * WW + j if i >= 0 and j >= 0 else -1)
    used = sorted(set(t for t in wanted if t >= 0))
    order = np.array(used + [t for t in range(FRAME) if t not in set(used)])
    place = np.argsort(order)
    return order, np.array([place[t] if t >= 0 else -1 for t in wanted])


ORDER, TAP_PLACE = tap_order()
GATHER = (ORDER[:, None] == np.arange(FRAME)[None, :]).astype(ml_dtypes.bfloat16)
TAP_GATHER = (TAP_PLACE[:, None] == np.arange(TAP_ROWS)[None, :]).astype(ml_dtypes.bfloat16)


def vmem(count):
    return [pl.BlockSpec(memory_space=pltpu.VMEM)] * count


def params(limit=20):
    return pltpu.CompilerParams(vmem_limit_bytes=limit * MB)


def cost(flops, moved, exps=0):
    return pl.CostEstimate(flops=int(flops), bytes_accessed=int(moved), transcendentals=int(exps))


def dot(a, b):
    return jnp.dot(a, b, preferred_element_type=jnp.float32)


def arrange_last_kernel(gather_ref, tokens_ref, last_ref):
    last_ref[...] = dot(gather_ref[...], tokens_ref[...]).astype(jnp.bfloat16)


def arrange_kernel(gather_ref, tokens_ref, w_out_ref, taps_ref, across_ref, beside_ref, own_ref):
    me = lax.axis_index("chan")
    frames = tokens_ref.shape[0] // FRAME
    count = frames * TAP_ROWS
    width = w_out_ref.shape[0]
    for f in range(frames):
        moved = dot(gather_ref[...], tokens_ref[f * FRAME : (f + 1) * FRAME, :]).astype(jnp.bfloat16)
        taps_ref[f * TAP_ROWS : (f + 1) * TAP_ROWS, :] = moved[:TAP_ROWS]
        across_ref[f * TAP_ROWS : (f + 1) * TAP_ROWS, :] = moved[TAP_ROWS:]
        beside_ref[f * TAP_ROWS : (f + 1) * TAP_ROWS, :] = moved[TAP_ROWS:]

    def columns(k):
        return w_out_ref[:, pl.ds(pl.multiple_of((me ^ k) * width, width), width)]

    own_ref[...] = columns(0)
    beside_ref[count:, :] = columns(1)
    across_ref[count : count + width, :] = columns(2)
    across_ref[count + width :, :] = columns(3)


def weight_rows(ref, me, k):
    width = ref.shape[0] // 4
    return ref[pl.ds(pl.multiple_of((me ^ k) * width, width), width), :]


def project(pieces, start, count, weights):
    total = dot(pieces[0][start : start + count, :], weights[0])
    for k in range(1, 4):
        total = total + dot(pieces[k][start : start + count, :], weights[k])
    return total


def tap_rows(rows, spread):
    return dot(spread, rows.astype(jnp.bfloat16))


def weigh(slabs, taps, first):
    total = None
    for q in range(9):
        term = slabs[q * POOL_ROWS : (q + 1) * POOL_ROWS] * taps[9 * first + q : 9 * first + q + 1, :]
        total = term if total is None else total + term
    return total


def group_mean(rows, averaging):
    high = rows.astype(jnp.bfloat16)
    rest = rows - high.astype(jnp.float32)
    middle = rest.astype(jnp.bfloat16)
    low = (rest - middle.astype(jnp.float32)).astype(jnp.bfloat16)
    return dot(high, averaging) + dot(middle, averaging) + dot(low, averaging)


def pool_kernel_body(
    a0, a1, a2, a3, l0, l1, l2, l3, wk_ref, wv_ref, taps_ref, spread_ref, out_ref
):
    me = lax.axis_index("chan")
    width = wk_ref.shape[1]
    lane = lax.broadcasted_iota(jnp.int32, (width, width), 1) // HDIM
    row = lax.broadcasted_iota(jnp.int32, (width, width), 0) // HDIM
    averaging = jnp.where(lane == row, 1.0 / HDIM, 0.0).astype(jnp.bfloat16)
    pooled_frames = out_ref.shape[0] // POOL_ROWS
    frames = 2 * pooled_frames
    for side, w_ref in enumerate((wk_ref, wv_ref)):
        weights = [weight_rows(w_ref, me, k) for k in range(4)]
        lanes = slice(side * width, (side + 1) * width)
        taps = taps_ref[:, lanes]
        sums = [None] * pooled_frames
        rows = project((l0, l1, l2, l3), 0, TAP_ROWS, weights)
        sums[0] = weigh(tap_rows(rows, spread_ref[...]), taps, 0)
        for f in range(frames):
            rows = project((a0, a1, a2, a3), f * TAP_ROWS, TAP_ROWS, weights)
            slabs = tap_rows(rows, spread_ref[...])
            t = f // 2
            part = weigh(slabs, taps, 1 + f % 2)
            sums[t] = part if sums[t] is None else sums[t] + part
            if f % 2 == 1 and t + 1 < pooled_frames:
                sums[t + 1] = weigh(slabs, taps, 0)
        for t in range(pooled_frames):
            center = sums[t] - group_mean(sums[t], averaging)
            spread = group_mean(center * center, averaging)
            out_ref[t * POOL_ROWS : (t + 1) * POOL_ROWS, lanes] = (center * lax.rsqrt(spread + EPSILON)).astype(
                jnp.bfloat16
            )


def tap_query_kernel(a0, a1, a2, a3, wq_ref, came_ref, after_ref, q_ref, *parts):
    del after_ref
    me = lax.axis_index("chan")
    weights = [weight_rows(wq_ref, me, k) for k in range(4)]
    for start in range(0, q_ref.shape[0], FRAME):
        rows = project((a0, a1, a2, a3), start, FRAME, weights)
        q_ref[start : start + FRAME, :] = rows.astype(jnp.bfloat16)
    at = 0
    for part in parts:
        part[...] = came_ref[at : at + part.shape[0], :]
        at += part.shape[0]


def query_kernel(q_ref, b0, b1, b2, c0, c1, wq_ref, back_ref, *rest):
    me = lax.axis_index("chan")
    outs, both = rest[:-1], rest[-1]
    weights = [weight_rows(wq_ref, me, k) for k in range(4)]
    frames = q_ref.shape[0] // TAP_ROWS
    places = [(ref, start) for ref in outs for start in range(0, ref.shape[0], FRAME)]
    for f in range(frames):
        both[f % 2, :TAP_ROWS, :] = q_ref[f * TAP_ROWS : (f + 1) * TAP_ROWS, :]
        at = f * TAP_ROWS
        others = dot(b0[at : at + TAP_ROWS, :], weights[0])
        for k, piece in ((1, b1), (2, b2)):
            others = others + dot(piece[at : at + TAP_ROWS, :], weights[k])
        far = c0 if f < frames // 2 else c1
        at = (f % (frames // 2)) * TAP_ROWS
        others = others + dot(far[at : at + TAP_ROWS, :], weights[3])
        both[f % 2, TAP_ROWS:, :] = others.astype(jnp.bfloat16)
        ref, start = places[f]
        ref[start : start + FRAME, :] = dot(back_ref[...], both[f % 2]).astype(jnp.bfloat16)


def row_kernel(own, b1, b2, b3, b4, b5, b6, b7, out_ref, head_ref, tail_ref):
    z = lax.rem(lax.axis_index("tm"), RING)
    block = own.shape[0]
    edge = head_ref.shape[0]
    for d, ref in enumerate((own, b1, b2, b3, b4, b5, b6, b7)):
        place = lax.rem(z + d, RING)
        out_ref[pl.ds(pl.multiple_of(place * block, block), block), :] = ref[...]
    head_ref[...] = out_ref[:edge, :]
    tail_ref[...] = out_ref[out_ref.shape[0] - edge :, :]


def attend_kernel(q_ref, before_ref, here_ref, after_ref, *rest):
    out_ref, window, keys, values = rest[-4:]
    width = q_ref.shape[1]
    heads = width // HDIM
    block = here_ref.shape[0] // RING
    count = keys.shape[1]
    z = lax.rem(lax.axis_index("tm"), RING)

    n = before_ref.shape[0]
    m = here_ref.shape[0]
    window[:n, :] = before_ref[...]
    window[n : n + m, :] = here_ref[...]
    window[n + m :, :] = after_ref[...]
    rows = window[pl.ds(pl.multiple_of(z * block, block), count), :]
    head = lax.broadcasted_iota(jnp.int32, (count, width), 1) // HDIM
    k = rows[:, :width].astype(jnp.float32) * (1.0 / math.sqrt(HDIM))
    v = rows[:, width:].astype(jnp.float32)
    for h in range(heads):
        keys[h] = jnp.where(head == h, k, 0.0).astype(jnp.bfloat16)
        values[h] = jnp.where(head == h, v, 0.0).astype(jnp.bfloat16)

    q = q_ref[...]
    total = q.astype(jnp.float32)
    for h in range(heads):
        scores = lax.dot_general(q, keys[h], (((1,), (1,)), ((), ())), preferred_element_type=jnp.float32)
        top = jnp.max(scores, axis=-1, keepdims=True)
        weighted = jnp.exp(scores - top)
        summed = jnp.sum(weighted, axis=-1, keepdims=True)
        total = total + dot(weighted.astype(jnp.bfloat16), values[h]) * (1.0 / summed)
    out_ref[...] = total.astype(jnp.bfloat16)


def out_kernel(a0, a1, a2, a3, w0, w1, w2, w3, tokens_ref, *rest):
    out_ref, done_ref = rest[-2:]
    done_ref[...] = jnp.zeros_like(done_ref)
    total = tokens_ref[...].astype(jnp.float32)
    acc = dot(a0[...], w0[...])
    for a, w in ((a1, w1), (a2, w2), (a3, w3)):
        acc = acc + dot(a[...], w[...])
    out_ref[...] = (total + acc).astype(jnp.bfloat16)


def swap(array, k):
    return lax.ppermute(array, "chan", [(i, i ^ k) for i in range(4)])


def ring_fetch(array, d, devices):
    return lax.ppermute(
        array, "tm", [(RING * (i // RING) + (i + d) % RING, i) for i in range(devices)]
    )


def per_device(tokens, w_query, w_key, w_value, w_out, pool_kernel):
    rows, width = tokens.shape
    frames = rows // FRAME
    devices = lax.axis_size("tm")
    bf16 = jnp.bfloat16
    gather = jnp.asarray(GATHER)
    back = jnp.asarray(np.ascontiguousarray(GATHER.T))
    tap_gather = jnp.asarray(TAP_GATHER)
    taps = jnp.concatenate(
        [jnp.tile(pool_kernel[0], (1, width // HDIM)), jnp.tile(pool_kernel[1], (1, width // HDIM))], axis=1
    )
    anywhere = pl.BlockSpec(memory_space=pl.ANY)

    last = pl.pallas_call(
        arrange_last_kernel,
        grid=(1,),
        out_shape=jax.ShapeDtypeStruct((TAP_ROWS, width), bf16),
        in_specs=[
            pl.BlockSpec((TAP_ROWS, FRAME), lambda s: (0, 0)),
            pl.BlockSpec((FRAME, width), lambda s: (frames - 1, 0)),
        ],
        out_specs=pl.BlockSpec((TAP_ROWS, width), lambda s: (0, 0)),
        compiler_params=params(),
        cost_estimate=cost(2 * TAP_ROWS * FRAME * width, 2 * FRAME * width),
        name="arrange_last",
    )(gather, tokens)
    last = lax.ppermute(last, "tm", [(i, (i + 1) % devices) for i in range(devices)])
    half = frames * TAP_ROWS
    body, rest_across, rest_beside, w_own = pl.pallas_call(
        arrange_kernel,
        out_shape=(
            jax.ShapeDtypeStruct((half, width), bf16),
            jax.ShapeDtypeStruct((half + 2 * width, width), bf16),
            jax.ShapeDtypeStruct((half + width, width), bf16),
            jax.ShapeDtypeStruct((width, width), bf16),
        ),
        in_specs=vmem(3),
        out_specs=tuple(vmem(4)),
        compiler_params=params(),
        cost_estimate=cost(2 * rows * FRAME * width, 4 * rows * width),
        name="arrange",
    )(gather, tokens, w_out)

    def spread(piece):
        across = swap(piece, 2)
        beside = swap(piece, 1)
        return piece, beside, across, swap(across, 1)

    body_pieces = spread(body)
    last_pieces = spread(last)
    rest_later, last_came = lax.optimization_barrier((rest_across, last_pieces[2]))
    last_pieces = (*last_pieces[:2], last_came, last_pieces[3])
    from_chip = swap(rest_later, 2)
    from_core = swap(rest_beside, 1)

    block = pl.pallas_call(
        pool_kernel_body,
        out_shape=jax.ShapeDtypeStruct((frames // 2 * POOL_ROWS, 2 * width), bf16),
        in_specs=vmem(12),
        out_specs=vmem(1)[0],
        compiler_params=params(),
        cost_estimate=cost(2 * frames * TAP_ROWS * D * 2 * width, 8 * rows * width),
        name="pool",
    )(*body_pieces, *last_pieces, w_key, w_value, taps, tap_gather)

    order = (1, 7, 2, 6, 3, 5, 4)
    by_place = {d: ring_fetch(block, d, devices) for d in order}
    edge = (RING - 2) * block.shape[0]
    ring, head, tail = pl.pallas_call(
        row_kernel,
        out_shape=tuple(jax.ShapeDtypeStruct((n, 2 * width), bf16) for n in (RING * block.shape[0], edge, edge)),
        in_specs=vmem(8),
        out_specs=tuple(vmem(3)),
        compiler_params=params(),
        cost_estimate=cost(0, 4 * RING * 2 * block.size),
        name="ring",
    )(block, *[by_place[d] for d in range(1, 8)])
    before = lax.ppermute(tail, "tm", [(i, (i + RING) % devices) for i in range(devices)])
    after = lax.ppermute(head, "tm", [((i + RING) % devices, i) for i in range(devices)])
    tap_queries, *onward = pl.pallas_call(
        tap_query_kernel,
        out_shape=tuple(jax.ShapeDtypeStruct((n, width), bf16) for n in (half, half // 2, half // 2, 2 * width)),
        in_specs=vmem(6) + [anywhere],
        out_specs=tuple(vmem(4)),
        compiler_params=params(),
        cost_estimate=cost(0, 0),
        name="tap_query",
    )(*body_pieces, w_query, from_chip, ring)
    from_far = [swap(piece, 1) for piece in onward]

    queries = pl.pallas_call(
        query_kernel,
        out_shape=tuple(jax.ShapeDtypeStruct((n * TILE, width), bf16) for n in CHUNKS),
        in_specs=vmem(8),
        out_specs=tuple(vmem(len(CHUNKS))),
        scratch_shapes=[pltpu.VMEM((2, FRAME, width), bf16)],
        compiler_params=params(),
        cost_estimate=cost(0, 0),
        name="query",
    )(
        tap_queries,
        rest_across,
        from_core,
        from_chip,
        from_far[0],
        from_far[1],
        w_query,
        back,
    )

    count = (2 * REACH + 1) * block.shape[0]
    heads = width // HDIM
    starts = [sum(CHUNKS[:i]) for i in range(len(CHUNKS))]
    first = half // width
    attended = []
    came = []
    marks = []
    result = None

    def attend(i):
        chunk = CHUNKS[i] * TILE
        waited = attended[-1:] + (marks[-1:] if i == 3 else []) + (came[i - 2 : i - 1] if i >= 2 else [])
        out = pl.pallas_call(
            attend_kernel,
            out_shape=jax.ShapeDtypeStruct((chunk, width), bf16),
            in_specs=vmem(4) + [anywhere] * len(waited),
            out_specs=vmem(1)[0],
            scratch_shapes=[
                pltpu.VMEM((2 * edge + ring.shape[0], 2 * width), bf16),
                pltpu.VMEM((heads, count, width), bf16),
                pltpu.VMEM((heads, count, width), bf16),
            ],
            compiler_params=params(36),
            cost_estimate=cost(0, 0),
            name=f"attend{i}",
        )(queries[i], before, ring, after, *waited)
        attended.append(out)
        came.append(swap(out, 2))
        return out, swap(out, 1), came[-1]

    def finish(i, pieces, result):
        own, beside, across = pieces[i]
        extra = () if result is None else (result,)
        if i + 2 < len(CHUNKS):
            onward, later = lax.optimization_barrier((across, pieces[i + 2][0]))
            pieces[i + 2] = (later, *pieces[i + 2][1:])
        else:
            onward, later = lax.optimization_barrier((across, marks[i - 2]))
            extra = (*extra, later)
        start, tiles = starts[i], CHUNKS[i]
        result, mark = pl.pallas_call(
            out_kernel,
            grid=(tiles,),
            out_shape=(jax.ShapeDtypeStruct((rows, width), bf16), jax.ShapeDtypeStruct((8, 128), jnp.float32)),
            in_specs=[pl.BlockSpec((TILE, width), lambda s: (s, 0))] * 4
            + [pl.BlockSpec((width, width), lambda s, at=at: (at, 0)) for at in (0, first, first, 1)]
            + [pl.BlockSpec((TILE, width), lambda s: (start + s, 0))]
            + [anywhere] * len(extra),
            out_specs=(
                pl.BlockSpec((TILE, width), lambda s: (start + s, 0)),
                pl.BlockSpec((8, 128), lambda s: (0, 0)),
            ),
            input_output_aliases={9: 0} if extra else {},
            compiler_params=params(),
            cost_estimate=cost(0, 0),
            name=f"out{i}",
        )(own, beside, across, swap(onward, 1), w_own, from_core, from_chip, from_far[2], tokens, *extra)
        marks.append(mark)
        return result

    pieces = [attend(i) for i in range(3)]
    for i in range(len(CHUNKS)):
        result = finish(i, pieces, result)
        if i + 3 < len(CHUNKS):
            pieces.append(attend(i + 3))
    return result


def solution(mesh):
    return jax.shard_map(
        per_device,
        mesh=mesh,
        in_specs=(
            P("tm", "chan"),
            P(None, "chan"),
            P(None, "chan"),
            P(None, "chan"),
            P("chan", None),
            P(),
        ),
        out_specs=P("tm", "chan"),
        check_vma=False,
    )
```

```python
import functools
import math

import jax
import jax.numpy as jnp
import ml_dtypes
import numpy as np
from jax import lax
from jax.experimental import pallas as pl
from jax.experimental.pallas import tpu as pltpu
from jax.sharding import PartitionSpec as P

D = 1024
HDIM = 64
HH = 16
WW = 16
FRAME = HH * WW
POOL_ROWS = (HH // 4) * (WW // 4)
TAP_ROWS = FRAME // 2
RING = 8
REACH = 6
TILE = 256
CHUNKS = (1, 2, 3, 2)
EPSILON = 1e-06
MB = 1024 * 1024


def tap_order():
    wanted = []
    for second in range(3):
        for third in range(3):
            for row in range(HH // 4):
                for col in range(WW // 4):
                    i, j = 4 * row - 1 + second, 4 * col - 1 + third
                    wanted.append(i * WW + j if i >= 0 and j >= 0 else -1)
    used = sorted(set(t for t in wanted if t >= 0))
    order = np.array(used + [t for t in range(FRAME) if t not in set(used)])
    place = np.argsort(order)
    return order, np.array([place[t] if t >= 0 else -1 for t in wanted])


ORDER, TAP_PLACE = tap_order()
TAP_GATHER = (TAP_PLACE[:, None] == np.arange(TAP_ROWS)[None, :]).astype(ml_dtypes.bfloat16)


def place_of(token):
    i, j = token // WW, token % WW
    rows_before, cols_before = i - (i + 1) // 4, j - (j + 1) // 4
    row_used = (i % 4 != 2) & (i != HH - 1)
    col_used = (j % 4 != 2) & (j != WW - 1)
    side = HH - 1 - HH // 4
    used_before = rows_before * side + jnp.where(row_used, cols_before, 0)
    return jnp.where(row_used & col_used, used_before, side * side + token - used_before)


def move_matrix(back):
    shape = (FRAME, FRAME)
    token = lax.broadcasted_iota(jnp.int32, shape, 0 if back else 1)
    place = lax.broadcasted_iota(jnp.int32, shape, 1 if back else 0)
    return jnp.where(place_of(token) == place, 1.0, 0.0).astype(jnp.bfloat16)


def vmem(count):
    return [pl.BlockSpec(memory_space=pltpu.VMEM)] * count


def params(limit=20):
    return pltpu.CompilerParams(vmem_limit_bytes=limit * MB)


def cost(flops, moved, exps=0):
    return pl.CostEstimate(flops=int(flops), bytes_accessed=int(moved), transcendentals=int(exps))


def dot(a, b):
    return jnp.dot(a, b, preferred_element_type=jnp.float32)


def arrange_kernel(
    tokens_hbm,
    w_out_hbm,
    wk_hbm,
    wv_hbm,
    wq_hbm,
    taps_ref,
    last_ref,
    across_ref,
    beside_ref,
    own_ref,
    key_value_ref,
    query_ref,
    tokens_ref,
    w_out_ref,
    frame_sems,
    w_sem,
    pack_sems,
):
    me = lax.axis_index("chan")
    frames = tokens_ref.shape[0] // FRAME
    count = frames * TAP_ROWS
    width = w_out_ref.shape[0]
    order = [frames - 1] + list(range(frames - 1))

    def frame_copy(f):
        rows = pl.ds(f * FRAME, FRAME)
        return pltpu.make_async_copy(tokens_hbm.at[rows, :], tokens_ref.at[rows, :], frame_sems.at[f])

    for f in order:
        frame_copy(f).start()
    w_copy = pltpu.make_async_copy(w_out_hbm, w_out_ref, w_sem)
    w_copy.start()
    copies = []
    for k in range(4):
        source = pl.ds(pl.multiple_of((me ^ k) * width, width), width)
        target = pl.ds(k * width, width)
        copies += [
            pltpu.make_async_copy(
                wk_hbm.at[source, :], key_value_ref.at[target, pl.ds(0, width)], pack_sems.at[3 * k]
            ),
            pltpu.make_async_copy(
                wv_hbm.at[source, :], key_value_ref.at[target, pl.ds(width, width)], pack_sems.at[3 * k + 1]
            ),
            pltpu.make_async_copy(wq_hbm.at[source, :], query_ref.at[target, :], pack_sems.at[3 * k + 2]),
        ]
    for copy in copies:
        copy.start()
    gather = move_matrix(False)
    for f in order:
        frame_copy(f).wait()
        moved = dot(gather, tokens_ref[f * FRAME : (f + 1) * FRAME, :]).astype(jnp.bfloat16)
        taps_ref[f * TAP_ROWS : (f + 1) * TAP_ROWS, :] = moved[:TAP_ROWS]
        if f == frames - 1:
            last_ref[...] = moved[:TAP_ROWS]
        across_ref[f * TAP_ROWS : (f + 1) * TAP_ROWS, :] = moved[TAP_ROWS:]
        beside_ref[f * TAP_ROWS : (f + 1) * TAP_ROWS, :] = moved[TAP_ROWS:]
    w_copy.wait()

    def columns(k):
        return w_out_ref[:, pl.ds(pl.multiple_of((me ^ k) * width, width), width)]

    own_ref[...] = columns(0)
    beside_ref[count:, :] = columns(1)
    across_ref[count : count + width, :] = columns(2)
    across_ref[count + width :, :] = columns(3)
    for copy in copies:
        copy.wait()


def project(pieces, start, count, weights):
    rows = jnp.concatenate([piece[start : start + count, :] for piece in pieces], axis=1)
    return dot(rows, weights).astype(jnp.bfloat16)


def weigh(slabs, taps, first):
    total = None
    for q in range(9):
        term = slabs[q * POOL_ROWS : (q + 1) * POOL_ROWS] * taps[9 * first + q : 9 * first + q + 1, :]
        total = term if total is None else total + term
    return total


def group_mean(rows, averaging):
    high = rows.astype(jnp.bfloat16)
    rest = rows - high.astype(jnp.float32)
    middle = rest.astype(jnp.bfloat16)
    low = (rest - middle.astype(jnp.float32)).astype(jnp.bfloat16)
    return dot(high, averaging) + dot(middle, averaging) + dot(low, averaging)


def pool_kernel_body(a0, a1, a2, a3, l0, l1, l2, l3, weights_ref, taps_ref, spread_ref, out_ref):
    width = weights_ref.shape[1] // 2
    lane = lax.broadcasted_iota(jnp.int32, (width, width), 1) // HDIM
    row = lax.broadcasted_iota(jnp.int32, (width, width), 0) // HDIM
    averaging = jnp.where(lane == row, 1.0 / HDIM, 0.0).astype(jnp.bfloat16)
    frames = a0.shape[0] // TAP_ROWS
    pooled_frames = frames // 2
    weights = weights_ref[...]
    taps = taps_ref[...]
    spread = spread_ref[...]
    sums = [None] * pooled_frames
    sums[0] = weigh(dot(spread, project((l0, l1, l2, l3), 0, TAP_ROWS, weights)), taps, 0)
    for f in range(frames):
        slabs = dot(spread, project((a0, a1, a2, a3), f * TAP_ROWS, TAP_ROWS, weights))
        t = f // 2
        part = weigh(slabs, taps, 1 + f % 2)
        sums[t] = part if sums[t] is None else sums[t] + part
        if f % 2 == 1 and t + 1 < pooled_frames:
            sums[t + 1] = weigh(slabs, taps, 0)
    pooled = jnp.concatenate(sums, axis=0)
    for side in range(2):
        lanes = slice(side * width, (side + 1) * width)
        center = pooled[:, lanes] - group_mean(pooled[:, lanes], averaging)
        spread_rows = group_mean(center * center, averaging)
        normal = (center * lax.rsqrt(spread_rows + EPSILON)).astype(jnp.bfloat16)
        for copy in range(out_ref.shape[0]):
            out_ref[copy, :, lanes] = normal


def tap_query_kernel(a0, a1, a2, a3, wq_ref, came_ref, after_ref, q_ref, *parts):
    del after_ref
    step = 2 * FRAME
    for start in range(0, q_ref.shape[0], step):
        q_ref[start : start + step, :] = project((a0, a1, a2, a3), start, step, wq_ref[...])
    at = 0
    for part in parts:
        part[...] = came_ref[at : at + part.shape[0], :]
        at += part.shape[0]


def query_kernel(q_ref, b0, b1, b2, c0, c1, wq_ref, *rest):
    outs, both = rest[:-1], rest[-1]
    frames = q_ref.shape[0] // TAP_ROWS
    back = move_matrix(True)
    places = [(ref, start) for ref in outs for start in range(0, ref.shape[0], FRAME)]
    far = c0.shape[0]
    for f in range(frames):
        at = f * TAP_ROWS
        both[f % 2, :TAP_ROWS, :] = q_ref[at : at + TAP_ROWS, :]
        c = c0 if at < far else c1
        pieces = [piece[at : at + TAP_ROWS, :] for piece in (b0, b1, b2)] + [c[at % far : at % far + TAP_ROWS, :]]
        others = dot(jnp.concatenate(pieces, axis=1), wq_ref[...])
        both[f % 2, TAP_ROWS:, :] = others.astype(jnp.bfloat16)
        ref, start = places[f]
        ref[start : start + FRAME, :] = dot(back, both[f % 2]).astype(jnp.bfloat16)


def ends_kernel(ring_ref, head_ref, tail_ref):
    edge = head_ref.shape[0]
    head_ref[...] = ring_ref[:edge, :]
    tail_ref[...] = ring_ref[ring_ref.shape[0] - edge :, :]


def attend_kernel(q_ref, before_ref, here_ref, after_ref, *rest):
    out_ref, window, keys, values = rest[-4:]
    width = q_ref.shape[1]
    heads = width // HDIM
    block = here_ref.shape[0] // RING
    count = keys.shape[1]
    z = lax.rem(lax.axis_index("tm"), RING)

    n = before_ref.shape[0]
    m = here_ref.shape[0]
    window[:n, :] = before_ref[...]
    window[n : n + m, :] = here_ref[...]
    window[n + m :, :] = after_ref[...]
    rows = window[pl.ds(pl.multiple_of(z * block, block), count), :]
    head = lax.broadcasted_iota(jnp.int32, (count, width), 1) // HDIM
    k = rows[:, :width].astype(jnp.float32) * (1.0 / math.sqrt(HDIM))
    v = rows[:, width:].astype(jnp.float32)
    for h in range(heads):
        keys[h] = jnp.where(head == h, k, 0.0).astype(jnp.bfloat16)
        values[h] = jnp.where(head == h, v, 0.0).astype(jnp.bfloat16)

    q = q_ref[...]
    total = q.astype(jnp.float32)
    for h in range(heads):
        scores = lax.dot_general(q, keys[h], (((1,), (1,)), ((), ())), preferred_element_type=jnp.float32)
        top = jnp.max(scores, axis=-1, keepdims=True)
        weighted = jnp.exp(scores - top)
        summed = jnp.sum(weighted, axis=-1, keepdims=True)
        total = total + dot(weighted.astype(jnp.bfloat16), values[h]) * (1.0 / summed)
    out_ref[...] = total.astype(jnp.bfloat16)


def out_kernel(a0, a1, a2, a3, w0, w1, w2, w3, tokens_ref, *rest):
    out_ref, done_ref = rest[-2:]
    done_ref[...] = jnp.zeros_like(done_ref)
    total = tokens_ref[...].astype(jnp.float32)
    acc = dot(a0[...], w0[...])
    for a, w in ((a1, w1), (a2, w2), (a3, w3)):
        acc = acc + dot(a[...], w[...])
    out_ref[...] = (total + acc).astype(jnp.bfloat16)


def swap(array, k):
    return lax.ppermute(array, "chan", [(i, i ^ k) for i in range(4)])


def per_device(tokens, w_query, w_key, w_value, w_out, pool_kernel):
    rows, width = tokens.shape
    frames = rows // FRAME
    devices = lax.axis_size("tm")
    bf16 = jnp.bfloat16
    tap_gather = jnp.asarray(TAP_GATHER)
    taps = jnp.concatenate(
        [jnp.tile(pool_kernel[0], (1, width // HDIM)), jnp.tile(pool_kernel[1], (1, width // HDIM))], axis=1
    )
    anywhere = pl.BlockSpec(memory_space=pl.ANY)

    hbm = pl.BlockSpec(memory_space=pltpu.HBM)
    half = frames * TAP_ROWS
    body, last, rest_across, rest_beside, w_own, key_value_weights, query_weights = pl.pallas_call(
        arrange_kernel,
        out_shape=(
            jax.ShapeDtypeStruct((half, width), bf16),
            jax.ShapeDtypeStruct((TAP_ROWS, width), bf16),
            jax.ShapeDtypeStruct((half + 2 * width, width), bf16),
            jax.ShapeDtypeStruct((half + width, width), bf16),
            jax.ShapeDtypeStruct((width, width), bf16),
            jax.ShapeDtypeStruct((D, 2 * width), bf16),
            jax.ShapeDtypeStruct((D, width), bf16),
        ),
        in_specs=[hbm] * 5,
        out_specs=tuple(vmem(5) + [anywhere, anywhere]),
        scratch_shapes=[
            pltpu.VMEM((rows, width), bf16),
            pltpu.VMEM((width, D), bf16),
            pltpu.SemaphoreType.DMA((frames,)),
            pltpu.SemaphoreType.DMA,
            pltpu.SemaphoreType.DMA((12,)),
        ],
        compiler_params=params(60),
        cost_estimate=cost(2 * rows * FRAME * width, 4 * rows * width),
        name="arrange",
    )(tokens, w_out, w_key, w_value, w_query)
    last = lax.ppermute(last, "tm", [(i, (i + 1) % devices) for i in range(devices)])

    last_across = swap(last, 2)
    body_across, last_across = lax.optimization_barrier((swap(body, 2), last_across))
    body_pieces = (body, swap(body, 1), body_across, swap(body_across, 1))
    last_pieces = (last, swap(last, 1), last_across, swap(last_across, 1))
    rest_later, last_came = lax.optimization_barrier((rest_across, last_pieces[2]))
    last_pieces = (*last_pieces[:2], last_came, last_pieces[3])
    from_chip = swap(rest_later, 2)
    from_core = swap(rest_beside, 1)

    block = pl.pallas_call(
        pool_kernel_body,
        out_shape=jax.ShapeDtypeStruct((RING, frames // 2 * POOL_ROWS, 2 * width), bf16),
        in_specs=vmem(11),
        out_specs=vmem(1)[0],
        compiler_params=params(),
        cost_estimate=cost(2 * frames * TAP_ROWS * D * 2 * width, 8 * rows * width),
        name="pool",
    )(*body_pieces, *last_pieces, key_value_weights, taps, tap_gather)

    block_rows = block.shape[1]
    rings = [[RING * r + z for z in range(RING)] for r in range(devices // RING)]
    ring = lax.all_to_all(block, "tm", 0, 0, axis_index_groups=rings).reshape(RING * block_rows, 2 * width)
    edge = (RING - 2) * block_rows
    head, tail = pl.pallas_call(
        ends_kernel,
        out_shape=(jax.ShapeDtypeStruct((edge, 2 * width), bf16), jax.ShapeDtypeStruct((edge, 2 * width), bf16)),
        in_specs=vmem(1),
        out_specs=tuple(vmem(2)),
        compiler_params=params(),
        cost_estimate=cost(0, 8 * edge * width),
        name="ends",
    )(ring)
    before = lax.ppermute(tail, "tm", [(i, (i + RING) % devices) for i in range(devices)])
    after = lax.ppermute(head, "tm", [((i + RING) % devices, i) for i in range(devices)])
    tap_queries, *onward = pl.pallas_call(
        tap_query_kernel,
        out_shape=tuple(jax.ShapeDtypeStruct((n, width), bf16) for n in (half, half // 2, half // 2, 2 * width)),
        in_specs=vmem(6) + [anywhere],
        out_specs=tuple(vmem(4)),
        compiler_params=params(),
        cost_estimate=cost(0, 0),
        name="tap_query",
    )(*body_pieces, query_weights, from_chip, ring)
    from_far = [swap(piece, 1) for piece in onward]

    queries = pl.pallas_call(
        query_kernel,
        out_shape=tuple(jax.ShapeDtypeStruct((n * TILE, width), bf16) for n in CHUNKS),
        in_specs=vmem(7),
        out_specs=tuple(vmem(len(CHUNKS))),
        scratch_shapes=[pltpu.VMEM((2, FRAME, width), bf16)],
        compiler_params=params(),
        cost_estimate=cost(0, 0),
        name="query",
    )(
        tap_queries,
        rest_across,
        from_core,
        from_chip,
        from_far[0],
        from_far[1],
        query_weights,
    )

    count = (2 * REACH + 1) * block_rows
    heads = width // HDIM
    starts = [sum(CHUNKS[:i]) for i in range(len(CHUNKS))]
    first = half // width
    attended = []
    came = []
    marks = []
    result = None

    def attend(i):
        chunk = CHUNKS[i] * TILE
        waited = attended[-1:] + (marks[-1:] if i == 3 else []) + (came[i - 2 : i - 1] if i >= 2 else [])
        out = pl.pallas_call(
            attend_kernel,
            out_shape=jax.ShapeDtypeStruct((chunk, width), bf16),
            in_specs=vmem(4) + [anywhere] * len(waited),
            out_specs=vmem(1)[0],
            scratch_shapes=[
                pltpu.VMEM((2 * edge + ring.shape[0], 2 * width), bf16),
                pltpu.VMEM((heads, count, width), bf16),
                pltpu.VMEM((heads, count, width), bf16),
            ],
            compiler_params=params(30),
            cost_estimate=cost(0, 0),
            name=f"attend{i}",
        )(queries[i], before, ring, after, *waited)
        attended.append(out)
        came.append(swap(out, 2))
        return out, swap(out, 1), came[-1]

    def finish(i, pieces, result):
        own, beside, across = pieces[i]
        extra = () if result is None else (result,)
        if i + 2 < len(CHUNKS):
            onward, later = lax.optimization_barrier((across, pieces[i + 2][0]))
            pieces[i + 2] = (later, *pieces[i + 2][1:])
        else:
            onward, later = lax.optimization_barrier((across, marks[i - 1]))
            extra = (*extra, later)
        start, tiles = starts[i], CHUNKS[i]
        result, mark = pl.pallas_call(
            out_kernel,
            grid=(tiles,),
            out_shape=(jax.ShapeDtypeStruct((rows, width), bf16), jax.ShapeDtypeStruct((8, 128), jnp.float32)),
            in_specs=[pl.BlockSpec((TILE, width), lambda s: (s, 0))] * 4
            + [pl.BlockSpec((width, width), lambda s, at=at: (at, 0)) for at in (0, first, first, 1)]
            + [pl.BlockSpec((TILE, width), lambda s: (start + s, 0))]
            + [anywhere] * len(extra),
            out_specs=(
                pl.BlockSpec((TILE, width), lambda s: (start + s, 0)),
                pl.BlockSpec((8, 128), lambda s: (0, 0)),
            ),
            input_output_aliases={9: 0} if extra else {},
            compiler_params=params(),
            cost_estimate=cost(0, 0),
            name=f"out{i}",
        )(own, beside, across, swap(onward, 1), w_own, from_core, from_chip, from_far[2], tokens, *extra)
        marks.append(mark)
        return result

    pieces = [attend(i) for i in range(3)]
    for i in range(len(CHUNKS)):
        result = finish(i, pieces, result)
        if i + 3 < len(CHUNKS):
            pieces.append(attend(i + 3))
    return result


def solution(mesh):
    return jax.shard_map(
        per_device,
        mesh=mesh,
        in_specs=(
            P("tm", "chan"),
            P(None, "chan"),
            P(None, "chan"),
            P(None, "chan"),
            P("chan", None),
            P(),
        ),
        out_specs=P("tm", "chan"),
        check_vma=False,
    )
```

```python
import functools
import math

import jax
import jax.numpy as jnp
import ml_dtypes
import numpy as np
from jax import lax
from jax.experimental import pallas as pl
from jax.experimental.pallas import tpu as pltpu
from jax.sharding import PartitionSpec as P

D = 1024
HDIM = 64
HH = 16
WW = 16
FRAME = HH * WW
POOL_ROWS = (HH // 4) * (WW // 4)
TAP_ROWS = FRAME // 2
RING = 8
REACH = 6
TILE = 256
CHUNKS = (1, 2, 2, 3)
EPSILON = 1e-06
MB = 1024 * 1024


def tap_order():
    wanted = []
    for second in range(3):
        for third in range(3):
            for row in range(HH // 4):
                for col in range(WW // 4):
                    i, j = 4 * row - 1 + second, 4 * col - 1 + third
                    wanted.append(i * WW + j if i >= 0 and j >= 0 else -1)
    used = sorted(set(t for t in wanted if t >= 0))
    order = np.array(used + [t for t in range(FRAME) if t not in set(used)])
    place = np.argsort(order)
    return order, np.array([place[t] if t >= 0 else -1 for t in wanted])


ORDER, TAP_PLACE = tap_order()
TAP_GATHER = (TAP_PLACE[:, None] == np.arange(TAP_ROWS)[None, :]).astype(ml_dtypes.bfloat16)


def place_of(token):
    i, j = token // WW, token % WW
    rows_before, cols_before = i - (i + 1) // 4, j - (j + 1) // 4
    row_used = (i % 4 != 2) & (i != HH - 1)
    col_used = (j % 4 != 2) & (j != WW - 1)
    side = HH - 1 - HH // 4
    used_before = rows_before * side + jnp.where(row_used, cols_before, 0)
    return jnp.where(row_used & col_used, used_before, side * side + token - used_before)


def move_matrix(back):
    shape = (FRAME, FRAME)
    token = lax.broadcasted_iota(jnp.int32, shape, 0 if back else 1)
    place = lax.broadcasted_iota(jnp.int32, shape, 1 if back else 0)
    return jnp.where(place_of(token) == place, 1.0, 0.0).astype(jnp.bfloat16)


def vmem(count):
    return [pl.BlockSpec(memory_space=pltpu.VMEM)] * count


def params(limit=20):
    return pltpu.CompilerParams(vmem_limit_bytes=limit * MB)


def cost(flops, moved, exps=0):
    return pl.CostEstimate(flops=int(flops), bytes_accessed=int(moved), transcendentals=int(exps))


def dot(a, b):
    return jnp.dot(a, b, preferred_element_type=jnp.float32)


def arrange_kernel(
    tokens_hbm, w_out_hbm, taps_ref, last_ref, across_ref, beside_ref, own_ref, tokens_ref, w_out_ref, frame_sems, w_sem
):
    me = lax.axis_index("chan")
    frames = tokens_ref.shape[0] // FRAME
    count = frames * TAP_ROWS
    width = w_out_ref.shape[0]
    order = [frames - 1] + list(range(frames - 1))

    def frame_copy(f):
        rows = pl.ds(f * FRAME, FRAME)
        return pltpu.make_async_copy(tokens_hbm.at[rows, :], tokens_ref.at[rows, :], frame_sems.at[f])

    for f in order:
        frame_copy(f).start()
    w_copy = pltpu.make_async_copy(w_out_hbm, w_out_ref, w_sem)
    w_copy.start()
    gather = move_matrix(False)
    for f in order:
        frame_copy(f).wait()
        moved = dot(gather, tokens_ref[f * FRAME : (f + 1) * FRAME, :]).astype(jnp.bfloat16)
        taps_ref[f * TAP_ROWS : (f + 1) * TAP_ROWS, :] = moved[:TAP_ROWS]
        if f == frames - 1:
            last_ref[...] = moved[:TAP_ROWS]
        across_ref[f * TAP_ROWS : (f + 1) * TAP_ROWS, :] = moved[TAP_ROWS:]
        beside_ref[f * TAP_ROWS : (f + 1) * TAP_ROWS, :] = moved[TAP_ROWS:]
    w_copy.wait()

    def columns(k):
        return w_out_ref[:, pl.ds(pl.multiple_of((me ^ k) * width, width), width)]

    own_ref[...] = columns(0)
    beside_ref[count:, :] = columns(1)
    across_ref[count : count + width, :] = columns(2)
    across_ref[count + width :, :] = columns(3)


def pack_kernel(wk_hbm, wv_hbm, wq_hbm, key_value_ref, query_ref, sems):
    me = lax.axis_index("chan")
    width = query_ref.shape[1]
    copies = []
    for k in range(4):
        source = pl.ds(pl.multiple_of((me ^ k) * width, width), width)
        target = pl.ds(k * width, width)
        copies += [
            pltpu.make_async_copy(
                wk_hbm.at[source, :], key_value_ref.at[target, pl.ds(0, width)], sems.at[3 * k]
            ),
            pltpu.make_async_copy(
                wv_hbm.at[source, :], key_value_ref.at[target, pl.ds(width, width)], sems.at[3 * k + 1]
            ),
            pltpu.make_async_copy(wq_hbm.at[source, :], query_ref.at[target, :], sems.at[3 * k + 2]),
        ]
    for copy in copies:
        copy.start()
    for copy in copies:
        copy.wait()


def project(pieces, start, count, weights):
    rows = jnp.concatenate([piece[start : start + count, :] for piece in pieces], axis=1)
    return dot(rows, weights).astype(jnp.bfloat16)


def weigh(slabs, taps, first):
    total = None
    for q in range(9):
        term = slabs[q * POOL_ROWS : (q + 1) * POOL_ROWS] * taps[9 * first + q : 9 * first + q + 1, :]
        total = term if total is None else total + term
    return total


def group_mean(rows, averaging):
    high = rows.astype(jnp.bfloat16)
    rest = rows - high.astype(jnp.float32)
    middle = rest.astype(jnp.bfloat16)
    low = (rest - middle.astype(jnp.float32)).astype(jnp.bfloat16)
    return dot(high, averaging) + dot(middle, averaging) + dot(low, averaging)


def pool_kernel_body(a0, a1, a2, a3, l0, l1, l2, l3, weights_ref, taps_ref, spread_ref, out_ref):
    width = weights_ref.shape[1] // 2
    lane = lax.broadcasted_iota(jnp.int32, (width, width), 1) // HDIM
    row = lax.broadcasted_iota(jnp.int32, (width, width), 0) // HDIM
    averaging = jnp.where(lane == row, 1.0 / HDIM, 0.0).astype(jnp.bfloat16)
    frames = a0.shape[0] // TAP_ROWS
    pooled_frames = frames // 2
    weights = weights_ref[...]
    taps = taps_ref[...]
    spread = spread_ref[...]
    sums = [None] * pooled_frames
    sums[0] = weigh(dot(spread, project((l0, l1, l2, l3), 0, TAP_ROWS, weights)), taps, 0)
    for f in range(frames):
        slabs = dot(spread, project((a0, a1, a2, a3), f * TAP_ROWS, TAP_ROWS, weights))
        t = f // 2
        part = weigh(slabs, taps, 1 + f % 2)
        sums[t] = part if sums[t] is None else sums[t] + part
        if f % 2 == 1 and t + 1 < pooled_frames:
            sums[t + 1] = weigh(slabs, taps, 0)
    pooled = jnp.concatenate(sums, axis=0)
    for side in range(2):
        lanes = slice(side * width, (side + 1) * width)
        center = pooled[:, lanes] - group_mean(pooled[:, lanes], averaging)
        spread_rows = group_mean(center * center, averaging)
        normal = (center * lax.rsqrt(spread_rows + EPSILON)).astype(jnp.bfloat16)
        for copy in range(out_ref.shape[0]):
            out_ref[copy, :, lanes] = normal


def tap_query_kernel(a0, a1, a2, a3, wq_ref, came_ref, after_ref, q_ref, *parts):
    del after_ref
    step = 2 * FRAME
    for start in range(0, q_ref.shape[0], step):
        q_ref[start : start + step, :] = project((a0, a1, a2, a3), start, step, wq_ref[...])
    at = 0
    for part in parts:
        part[...] = came_ref[at : at + part.shape[0], :]
        at += part.shape[0]


def query_kernel(q_ref, b0, b1, b2, c0, c1, wq_ref, *rest):
    outs, both = rest[:-1], rest[-1]
    frames = q_ref.shape[0] // TAP_ROWS
    back = move_matrix(True)
    places = [(ref, start) for ref in outs for start in range(0, ref.shape[0], FRAME)]
    far = c0.shape[0]
    for f in range(frames):
        at = f * TAP_ROWS
        both[f % 2, :TAP_ROWS, :] = q_ref[at : at + TAP_ROWS, :]
        c = c0 if at < far else c1
        pieces = [piece[at : at + TAP_ROWS, :] for piece in (b0, b1, b2)] + [c[at % far : at % far + TAP_ROWS, :]]
        others = dot(jnp.concatenate(pieces, axis=1), wq_ref[...])
        both[f % 2, TAP_ROWS:, :] = others.astype(jnp.bfloat16)
        ref, start = places[f]
        ref[start : start + FRAME, :] = dot(back, both[f % 2]).astype(jnp.bfloat16)


def ends_kernel(ring_ref, head_ref, tail_ref):
    edge = head_ref.shape[0]
    head_ref[...] = ring_ref[:edge, :]
    tail_ref[...] = ring_ref[ring_ref.shape[0] - edge :, :]


def attend_kernel(q_ref, before_ref, here_ref, after_ref, *rest):
    out_ref, window, keys, values = rest[-4:]
    width = q_ref.shape[1]
    heads = width // HDIM
    block = here_ref.shape[0] // RING
    count = keys.shape[1]
    z = lax.rem(lax.axis_index("tm"), RING)

    n = before_ref.shape[0]
    m = here_ref.shape[0]
    window[:n, :] = before_ref[...]
    window[n : n + m, :] = here_ref[...]
    window[n + m :, :] = after_ref[...]
    rows = window[pl.ds(pl.multiple_of(z * block, block), count), :]
    head = lax.broadcasted_iota(jnp.int32, (count, width), 1) // HDIM
    k = rows[:, :width].astype(jnp.float32) * (1.0 / math.sqrt(HDIM))
    v = rows[:, width:].astype(jnp.float32)
    for h in range(heads):
        keys[h] = jnp.where(head == h, k, 0.0).astype(jnp.bfloat16)
        values[h] = jnp.where(head == h, v, 0.0).astype(jnp.bfloat16)

    q = q_ref[...]
    total = q.astype(jnp.float32)
    for h in range(heads):
        scores = lax.dot_general(q, keys[h], (((1,), (1,)), ((), ())), preferred_element_type=jnp.float32)
        top = jnp.max(scores, axis=-1, keepdims=True)
        weighted = jnp.exp(scores - top)
        summed = jnp.sum(weighted, axis=-1, keepdims=True)
        total = total + dot(weighted.astype(jnp.bfloat16), values[h]) * (1.0 / summed)
    out_ref[...] = total.astype(jnp.bfloat16)


def out_kernel(a0, a1, a2, a3, w0, w1, w2, w3, tokens_ref, *rest):
    out_ref, done_ref = rest[-2:]
    done_ref[...] = jnp.zeros_like(done_ref)
    total = tokens_ref[...].astype(jnp.float32)
    acc = dot(a0[...], w0[...])
    for a, w in ((a1, w1), (a2, w2), (a3, w3)):
        acc = acc + dot(a[...], w[...])
    out_ref[...] = (total + acc).astype(jnp.bfloat16)


def swap(array, k):
    return lax.ppermute(array, "chan", [(i, i ^ k) for i in range(4)])


def per_device(tokens, w_query, w_key, w_value, w_out, pool_kernel):
    rows, width = tokens.shape
    frames = rows // FRAME
    devices = lax.axis_size("tm")
    bf16 = jnp.bfloat16
    tap_gather = jnp.asarray(TAP_GATHER)
    taps = jnp.concatenate(
        [jnp.tile(pool_kernel[0], (1, width // HDIM)), jnp.tile(pool_kernel[1], (1, width // HDIM))], axis=1
    )
    anywhere = pl.BlockSpec(memory_space=pl.ANY)

    hbm = pl.BlockSpec(memory_space=pltpu.HBM)
    half = frames * TAP_ROWS
    body, last, rest_across, rest_beside, w_own = pl.pallas_call(
        arrange_kernel,
        out_shape=(
            jax.ShapeDtypeStruct((half, width), bf16),
            jax.ShapeDtypeStruct((TAP_ROWS, width), bf16),
            jax.ShapeDtypeStruct((half + 2 * width, width), bf16),
            jax.ShapeDtypeStruct((half + width, width), bf16),
            jax.ShapeDtypeStruct((width, width), bf16),
        ),
        in_specs=[hbm] * 2,
        out_specs=tuple(vmem(5)),
        scratch_shapes=[
            pltpu.VMEM((rows, width), bf16),
            pltpu.VMEM((width, D), bf16),
            pltpu.SemaphoreType.DMA((frames,)),
            pltpu.SemaphoreType.DMA,
        ],
        compiler_params=params(60),
        cost_estimate=cost(2 * rows * FRAME * width, 4 * rows * width),
        name="arrange",
    )(tokens, w_out)
    key_value_weights, query_weights = pl.pallas_call(
        pack_kernel,
        out_shape=(jax.ShapeDtypeStruct((D, 2 * width), bf16), jax.ShapeDtypeStruct((D, width), bf16)),
        in_specs=[hbm] * 3,
        out_specs=tuple(vmem(2)),
        scratch_shapes=[pltpu.SemaphoreType.DMA((12,))],
        compiler_params=params(8),
        cost_estimate=cost(0, 12 * D * width),
        name="pack",
    )(w_key, w_value, w_query)
    last = lax.ppermute(last, "tm", [(i, (i + 1) % devices) for i in range(devices)])

    last, key_value_weights = lax.optimization_barrier((last, key_value_weights))
    last_across = swap(last, 2)
    body_across, last_across = lax.optimization_barrier((swap(body, 2), last_across))
    body_pieces = (body, swap(body, 1), body_across, swap(body_across, 1))
    last_pieces = (last, swap(last, 1), last_across, swap(last_across, 1))
    rest_later, last_came = lax.optimization_barrier((rest_across, last_pieces[2]))
    last_pieces = (*last_pieces[:2], last_came, last_pieces[3])
    from_chip = swap(rest_later, 2)
    from_core = swap(rest_beside, 1)

    block = pl.pallas_call(
        pool_kernel_body,
        out_shape=jax.ShapeDtypeStruct((RING, frames // 2 * POOL_ROWS, 2 * width), bf16),
        in_specs=vmem(11),
        out_specs=vmem(1)[0],
        compiler_params=params(),
        cost_estimate=cost(2 * frames * TAP_ROWS * D * 2 * width, 8 * rows * width),
        name="pool",
    )(*body_pieces, *last_pieces, key_value_weights, taps, tap_gather)

    block_rows = block.shape[1]
    rings = [[RING * r + z for z in range(RING)] for r in range(devices // RING)]
    ring = lax.all_to_all(block, "tm", 0, 0, axis_index_groups=rings).reshape(RING * block_rows, 2 * width)
    edge = (RING - 2) * block_rows
    head, tail = pl.pallas_call(
        ends_kernel,
        out_shape=(jax.ShapeDtypeStruct((edge, 2 * width), bf16), jax.ShapeDtypeStruct((edge, 2 * width), bf16)),
        in_specs=vmem(1),
        out_specs=tuple(vmem(2)),
        compiler_params=params(),
        cost_estimate=cost(0, 8 * edge * width),
        name="ends",
    )(ring)
    before = lax.ppermute(tail, "tm", [(i, (i + RING) % devices) for i in range(devices)])
    after = lax.ppermute(head, "tm", [((i + RING) % devices, i) for i in range(devices)])
    tap_queries, *onward = pl.pallas_call(
        tap_query_kernel,
        out_shape=tuple(jax.ShapeDtypeStruct((n, width), bf16) for n in (half, half // 2, half // 2, 2 * width)),
        in_specs=vmem(6) + [anywhere],
        out_specs=tuple(vmem(4)),
        compiler_params=params(),
        cost_estimate=cost(0, 0),
        name="tap_query",
    )(*body_pieces, query_weights, from_chip, ring)
    from_far = [swap(piece, 1) for piece in onward]

    queries = pl.pallas_call(
        query_kernel,
        out_shape=tuple(jax.ShapeDtypeStruct((n * TILE, width), bf16) for n in CHUNKS),
        in_specs=vmem(7),
        out_specs=tuple(vmem(len(CHUNKS))),
        scratch_shapes=[pltpu.VMEM((2, FRAME, width), bf16)],
        compiler_params=params(),
        cost_estimate=cost(0, 0),
        name="query",
    )(
        tap_queries,
        rest_across,
        from_core,
        from_chip,
        from_far[0],
        from_far[1],
        query_weights,
    )

    count = (2 * REACH + 1) * block_rows
    heads = width // HDIM
    starts = [sum(CHUNKS[:i]) for i in range(len(CHUNKS))]
    first = half // width
    attended = []
    came = []
    marks = []
    result = None

    def attend(i):
        chunk = CHUNKS[i] * TILE
        waited = attended[-1:] + (marks[-1:] if i == 3 else []) + (came[i - 2 : i - 1] if i >= 2 else [])
        out = pl.pallas_call(
            attend_kernel,
            out_shape=jax.ShapeDtypeStruct((chunk, width), bf16),
            in_specs=vmem(4) + [anywhere] * len(waited),
            out_specs=vmem(1)[0],
            scratch_shapes=[
                pltpu.VMEM((2 * edge + ring.shape[0], 2 * width), bf16),
                pltpu.VMEM((heads, count, width), bf16),
                pltpu.VMEM((heads, count, width), bf16),
            ],
            compiler_params=params(30),
            cost_estimate=cost(0, 0),
            name=f"attend{i}",
        )(queries[i], before, ring, after, *waited)
        attended.append(out)
        came.append(swap(out, 2))
        return out, swap(out, 1), came[-1]

    def finish(i, pieces, result):
        own, beside, across = pieces[i]
        extra = () if result is None else (result,)
        n = min(i + 2, len(CHUNKS) - 1)
        if i < n:
            onward, later = lax.optimization_barrier((across, pieces[n][0]))
            pieces[n] = (later, *pieces[n][1:])
        else:
            onward, later = lax.optimization_barrier((across, marks[i - 1]))
            extra = (*extra, later)
        start, tiles = starts[i], CHUNKS[i]
        result, mark = pl.pallas_call(
            out_kernel,
            grid=(tiles,),
            out_shape=(jax.ShapeDtypeStruct((rows, width), bf16), jax.ShapeDtypeStruct((8, 128), jnp.float32)),
            in_specs=[pl.BlockSpec((TILE, width), lambda s: (s, 0))] * 4
            + [pl.BlockSpec((width, width), lambda s, at=at: (at, 0)) for at in (0, first, first, 1)]
            + [pl.BlockSpec((TILE, width), lambda s: (start + s, 0))]
            + [anywhere] * len(extra),
            out_specs=(
                pl.BlockSpec((TILE, width), lambda s: (start + s, 0)),
                pl.BlockSpec((8, 128), lambda s: (0, 0)),
            ),
            input_output_aliases={9: 0} if extra else {},
            compiler_params=params(),
            cost_estimate=cost(0, 0),
            name=f"out{i}",
        )(own, beside, across, swap(onward, 1), w_own, from_core, from_chip, from_far[2], tokens, *extra)
        marks.append(mark)
        return result

    pieces = [attend(i) for i in range(3)]
    for i in range(len(CHUNKS)):
        result = finish(i, pieces, result)
        if i + 3 < len(CHUNKS):
            pieces.append(attend(i + 3))
    return result


def solution(mesh):
    return jax.shard_map(
        per_device,
        mesh=mesh,
        in_specs=(
            P("tm", "chan"),
            P(None, "chan"),
            P(None, "chan"),
            P(None, "chan"),
            P("chan", None),
            P(),
        ),
        out_specs=P("tm", "chan"),
        check_vma=False,
    )
```

```python
import functools
import math

import jax
import jax.numpy as jnp
import ml_dtypes
import numpy as np
from jax import lax
from jax.experimental import pallas as pl
from jax.experimental.pallas import tpu as pltpu
from jax.sharding import PartitionSpec as P

D = 1024
HDIM = 64
HH = 16
WW = 16
FRAME = HH * WW
POOL_ROWS = (HH // 4) * (WW // 4)
TAP_ROWS = FRAME // 2
RING = 8
REACH = 6
TILE = 256
CHUNKS = (1, 2, 2, 3)
EPSILON = 1e-06
MB = 1024 * 1024


def tap_order():
    wanted = []
    for second in range(3):
        for third in range(3):
            for row in range(HH // 4):
                for col in range(WW // 4):
                    i, j = 4 * row - 1 + second, 4 * col - 1 + third
                    wanted.append(i * WW + j if i >= 0 and j >= 0 else -1)
    used = sorted(set(t for t in wanted if t >= 0))
    order = np.array(used + [t for t in range(FRAME) if t not in set(used)])
    place = np.argsort(order)
    return order, np.array([place[t] if t >= 0 else -1 for t in wanted])


ORDER, TAP_PLACE = tap_order()
TAP_GATHER = (TAP_PLACE[:, None] == np.arange(TAP_ROWS)[None, :]).astype(ml_dtypes.bfloat16)


def place_of(token):
    i, j = token // WW, token % WW
    rows_before, cols_before = i - (i + 1) // 4, j - (j + 1) // 4
    row_used = (i % 4 != 2) & (i != HH - 1)
    col_used = (j % 4 != 2) & (j != WW - 1)
    side = HH - 1 - HH // 4
    used_before = rows_before * side + jnp.where(row_used, cols_before, 0)
    return jnp.where(row_used & col_used, used_before, side * side + token - used_before)


def move_matrix(back):
    token = lax.broadcasted_iota(jnp.int32, (FRAME, 1) if back else (1, FRAME), 0 if back else 1)
    place = lax.broadcasted_iota(jnp.int32, (FRAME, FRAME), 1 if back else 0)
    return jnp.where(place_of(token) == place, 1.0, 0.0).astype(jnp.bfloat16)


def vmem(count):
    return [pl.BlockSpec(memory_space=pltpu.VMEM)] * count


def params(limit=20):
    return pltpu.CompilerParams(vmem_limit_bytes=limit * MB)


def cost(flops, moved, exps=0):
    return pl.CostEstimate(flops=int(flops), bytes_accessed=int(moved), transcendentals=int(exps))


def dot(a, b):
    return jnp.dot(a, b, preferred_element_type=jnp.float32)


def arrange_kernel(
    tokens_hbm, w_out_hbm, taps_ref, last_ref, across_ref, beside_ref, own_ref, tokens_ref, w_out_ref, frame_sems, w_sem
):
    me = lax.axis_index("chan")
    frames = tokens_ref.shape[0] // FRAME
    count = frames * TAP_ROWS
    width = w_out_ref.shape[0]
    order = [frames - 1] + list(range(frames - 1))

    def frame_copy(f):
        rows = pl.ds(f * FRAME, FRAME)
        return pltpu.make_async_copy(tokens_hbm.at[rows, :], tokens_ref.at[rows, :], frame_sems.at[f])

    for f in order:
        frame_copy(f).start()
    w_copy = pltpu.make_async_copy(w_out_hbm, w_out_ref, w_sem)
    w_copy.start()
    gather = move_matrix(False)
    for f in order:
        frame_copy(f).wait()
        moved = dot(gather, tokens_ref[f * FRAME : (f + 1) * FRAME, :]).astype(jnp.bfloat16)
        taps_ref[f * TAP_ROWS : (f + 1) * TAP_ROWS, :] = moved[:TAP_ROWS]
        if f == frames - 1:
            last_ref[...] = moved[:TAP_ROWS]
        across_ref[f * TAP_ROWS : (f + 1) * TAP_ROWS, :] = moved[TAP_ROWS:]
        beside_ref[f * TAP_ROWS : (f + 1) * TAP_ROWS, :] = moved[TAP_ROWS:]
    w_copy.wait()

    def columns(k):
        return w_out_ref[:, pl.ds(pl.multiple_of((me ^ k) * width, width), width)]

    own_ref[...] = columns(0)
    beside_ref[count:, :] = columns(1)
    across_ref[count : count + width, :] = columns(2)
    across_ref[count + width :, :] = columns(3)


def pack_kernel(wk_hbm, wv_hbm, wq_hbm, pool_ref, key_value_ref, query_ref, taps_ref, sems):
    me = lax.axis_index("chan")
    width = query_ref.shape[1]
    copies = []
    for k in range(4):
        source = pl.ds(pl.multiple_of((me ^ k) * width, width), width)
        target = pl.ds(k * width, width)
        copies += [
            pltpu.make_async_copy(
                wk_hbm.at[source, :], key_value_ref.at[target, pl.ds(0, width)], sems.at[3 * k]
            ),
            pltpu.make_async_copy(
                wv_hbm.at[source, :], key_value_ref.at[target, pl.ds(width, width)], sems.at[3 * k + 1]
            ),
            pltpu.make_async_copy(wq_hbm.at[source, :], query_ref.at[target, :], sems.at[3 * k + 2]),
        ]
    for copy in copies:
        copy.start()
    heads = width // HDIM
    taps_ref[...] = jnp.concatenate([pool_ref[0]] * heads + [pool_ref[1]] * heads, axis=1)
    for copy in copies:
        copy.wait()


def project(pieces, start, count, weights):
    rows = jnp.concatenate([piece[start : start + count, :] for piece in pieces], axis=1)
    return dot(rows, weights).astype(jnp.bfloat16)


def weigh(slabs, taps, first):
    total = None
    for q in range(9):
        term = slabs[q * POOL_ROWS : (q + 1) * POOL_ROWS] * taps[9 * first + q : 9 * first + q + 1, :]
        total = term if total is None else total + term
    return total


def group_mean(rows, averaging):
    high = rows.astype(jnp.bfloat16)
    rest = rows - high.astype(jnp.float32)
    middle = rest.astype(jnp.bfloat16)
    low = (rest - middle.astype(jnp.float32)).astype(jnp.bfloat16)
    return dot(high, averaging) + dot(middle, averaging) + dot(low, averaging)


def pool_kernel_body(a0, a1, a2, a3, l0, l1, l2, l3, weights_ref, taps_ref, spread_ref, out_ref):
    width = weights_ref.shape[1] // 2
    lane = lax.broadcasted_iota(jnp.int32, (width, width), 1) // HDIM
    row = lax.broadcasted_iota(jnp.int32, (width, width), 0) // HDIM
    averaging = jnp.where(lane == row, 1.0 / HDIM, 0.0).astype(jnp.bfloat16)
    frames = a0.shape[0] // TAP_ROWS
    pooled_frames = frames // 2
    weights = weights_ref[...]
    taps = taps_ref[...]
    spread = spread_ref[...]
    sums = [None] * pooled_frames
    sums[0] = weigh(dot(spread, project((l0, l1, l2, l3), 0, TAP_ROWS, weights)), taps, 0)
    for f in range(frames):
        slabs = dot(spread, project((a0, a1, a2, a3), f * TAP_ROWS, TAP_ROWS, weights))
        t = f // 2
        part = weigh(slabs, taps, 1 + f % 2)
        sums[t] = part if sums[t] is None else sums[t] + part
        if f % 2 == 1 and t + 1 < pooled_frames:
            sums[t + 1] = weigh(slabs, taps, 0)
    pooled = jnp.concatenate(sums, axis=0)
    for side in range(2):
        lanes = slice(side * width, (side + 1) * width)
        center = pooled[:, lanes] - group_mean(pooled[:, lanes], averaging)
        spread_rows = group_mean(center * center, averaging)
        normal = (center * lax.rsqrt(spread_rows + EPSILON)).astype(jnp.bfloat16)
        out_ref[:, lanes] = normal


def tap_query_kernel(a0, a1, a2, a3, wq_ref, came_ref, after_ref, q_ref, *parts):
    del after_ref
    step = 2 * FRAME
    for start in range(0, q_ref.shape[0], step):
        q_ref[start : start + step, :] = project((a0, a1, a2, a3), start, step, wq_ref[...])
    at = 0
    for part in parts:
        part[...] = came_ref[at : at + part.shape[0], :]
        at += part.shape[0]


def query_kernel(q_ref, b0, b1, b2, c0, c1, wq_ref, *rest):
    outs, both = rest[:-1], rest[-1]
    frames = q_ref.shape[0] // TAP_ROWS
    back = move_matrix(True)
    places = [(ref, start) for ref in outs for start in range(0, ref.shape[0], FRAME)]
    far = c0.shape[0]
    for f in range(frames):
        at = f * TAP_ROWS
        both[f % 2, :TAP_ROWS, :] = q_ref[at : at + TAP_ROWS, :]
        c = c0 if at < far else c1
        pieces = [piece[at : at + TAP_ROWS, :] for piece in (b0, b1, b2)] + [c[at % far : at % far + TAP_ROWS, :]]
        others = dot(jnp.concatenate(pieces, axis=1), wq_ref[...])
        both[f % 2, TAP_ROWS:, :] = others.astype(jnp.bfloat16)
        ref, start = places[f]
        ref[start : start + FRAME, :] = dot(back, both[f % 2]).astype(jnp.bfloat16)


def pair_kernel(own_ref, peer_ref, both_ref):
    block = own_ref.shape[0]
    both_ref[:block, :] = own_ref[...]
    both_ref[block:, :] = peer_ref[...]


def ring_kernel(own, far, r1, r2, r3, s1, s2, s3, ring_ref, head_ref, tail_ref):
    z = lax.rem(lax.axis_index("tm"), RING)
    core = lax.rem(lax.axis_index("chan"), 2)
    block = own.shape[0]
    edge = head_ref.shape[0]

    def put(place, value):
        ring_ref[pl.ds(pl.multiple_of(lax.rem(place, RING) * block, block), block), :] = value

    put(z, own[...])
    put(z + RING // 2, far[...])
    for d, r, s in ((1, r1, s1), (2, r2, s2), (3, r3, s3)):
        step = d + core * (RING - 2 * d)
        put(z + step, r[:block, :])
        put(z + RING - step, s[block:, :])
    head_ref[...] = ring_ref[:edge, :]
    tail_ref[...] = ring_ref[ring_ref.shape[0] - edge :, :]


def attend_kernel(q_ref, before_ref, here_ref, after_ref, *rest):
    out_ref, window, keys, values = rest[-4:]
    width = q_ref.shape[1]
    heads = width // HDIM
    block = here_ref.shape[0] // RING
    count = keys.shape[1]
    z = lax.rem(lax.axis_index("tm"), RING)

    n = before_ref.shape[0]
    m = here_ref.shape[0]
    window[:n, :] = before_ref[...]
    window[n : n + m, :] = here_ref[...]
    window[n + m :, :] = after_ref[...]
    rows = window[pl.ds(pl.multiple_of(z * block, block), count), :]
    head = lax.broadcasted_iota(jnp.int32, (count, width), 1) // HDIM
    k = rows[:, :width].astype(jnp.float32) * (1.0 / math.sqrt(HDIM))
    v = rows[:, width:].astype(jnp.float32)
    for h in range(heads):
        keys[h] = jnp.where(head == h, k, 0.0).astype(jnp.bfloat16)
        values[h] = jnp.where(head == h, v, 0.0).astype(jnp.bfloat16)

    q = q_ref[...]
    total = q.astype(jnp.float32)
    for h in range(heads):
        scores = lax.dot_general(q, keys[h], (((1,), (1,)), ((), ())), preferred_element_type=jnp.float32)
        top = jnp.max(scores, axis=-1, keepdims=True)
        weighted = jnp.exp(scores - top)
        summed = jnp.sum(weighted, axis=-1, keepdims=True)
        total = total + dot(weighted.astype(jnp.bfloat16), values[h]) * (1.0 / summed)
    out_ref[...] = total.astype(jnp.bfloat16)


def out_kernel(a0, a1, a2, a3, w0, w1, w2, w3, tokens_ref, *rest):
    out_ref, done_ref = rest[-2:]
    done_ref[...] = jnp.zeros_like(done_ref)
    total = tokens_ref[...].astype(jnp.float32)
    acc = dot(a0[...], w0[...])
    for a, w in ((a1, w1), (a2, w2), (a3, w3)):
        acc = acc + dot(a[...], w[...])
    out_ref[...] = (total + acc).astype(jnp.bfloat16)


def swap(array, k):
    return lax.ppermute(array, "chan", [(i, i ^ k) for i in range(4)])


def per_device(tokens, w_query, w_key, w_value, w_out, pool_kernel):
    rows, width = tokens.shape
    frames = rows // FRAME
    devices = lax.axis_size("tm")
    bf16 = jnp.bfloat16
    tap_gather = jnp.asarray(TAP_GATHER)
    anywhere = pl.BlockSpec(memory_space=pl.ANY)

    hbm = pl.BlockSpec(memory_space=pltpu.HBM)
    half = frames * TAP_ROWS
    body, last, rest_across, rest_beside, w_own = pl.pallas_call(
        arrange_kernel,
        out_shape=(
            jax.ShapeDtypeStruct((half, width), bf16),
            jax.ShapeDtypeStruct((TAP_ROWS, width), bf16),
            jax.ShapeDtypeStruct((half + 2 * width, width), bf16),
            jax.ShapeDtypeStruct((half + width, width), bf16),
            jax.ShapeDtypeStruct((width, width), bf16),
        ),
        in_specs=[hbm] * 2,
        out_specs=tuple(vmem(5)),
        scratch_shapes=[
            pltpu.VMEM((rows, width), bf16),
            pltpu.VMEM((width, D), bf16),
            pltpu.SemaphoreType.DMA((frames,)),
            pltpu.SemaphoreType.DMA,
        ],
        compiler_params=params(60),
        cost_estimate=cost(2 * rows * FRAME * width, 4 * rows * width),
        name="arrange",
    )(tokens, w_out)
    key_value_weights, query_weights, taps = pl.pallas_call(
        pack_kernel,
        out_shape=(
            jax.ShapeDtypeStruct((D, 2 * width), bf16),
            jax.ShapeDtypeStruct((D, width), bf16),
            jax.ShapeDtypeStruct((pool_kernel.shape[1], 2 * width), jnp.float32),
        ),
        in_specs=[hbm] * 3 + vmem(1),
        out_specs=tuple(vmem(3)),
        scratch_shapes=[pltpu.SemaphoreType.DMA((12,))],
        compiler_params=params(8),
        cost_estimate=cost(0, 12 * D * width),
        name="pack",
    )(w_key, w_value, w_query, pool_kernel)
    last = lax.ppermute(last, "tm", [(i, (i + 1) % devices) for i in range(devices)])

    last, key_value_weights = lax.optimization_barrier((last, key_value_weights))
    last_across = swap(last, 2)
    body_across, last_across = lax.optimization_barrier((swap(body, 2), last_across))
    body_pieces = (body, swap(body, 1), body_across, swap(body_across, 1))
    last_pieces = (last, swap(last, 1), last_across, swap(last_across, 1))
    rest_later, last_came = lax.optimization_barrier((rest_across, last_pieces[2]))
    last_pieces = (*last_pieces[:2], last_came, last_pieces[3])
    from_chip = swap(rest_later, 2)
    from_core = swap(rest_beside, 1)

    block = pl.pallas_call(
        pool_kernel_body,
        out_shape=jax.ShapeDtypeStruct((frames // 2 * POOL_ROWS, 2 * width), bf16),
        in_specs=vmem(11),
        out_specs=vmem(1)[0],
        compiler_params=params(),
        cost_estimate=cost(2 * frames * TAP_ROWS * D * 2 * width, 8 * rows * width),
        name="pool",
    )(*body_pieces, *last_pieces, key_value_weights, taps, tap_gather)

    block_rows = block.shape[0]
    far = lax.ppermute(
        block, "tm", [(RING * (i // RING) + (i + RING // 2) % RING, i) for i in range(devices)]
    )
    both = pl.pallas_call(
        pair_kernel,
        out_shape=jax.ShapeDtypeStruct((2 * block_rows, 2 * width), bf16),
        in_specs=vmem(2),
        out_specs=vmem(1)[0],
        compiler_params=params(4),
        cost_estimate=cost(0, 0),
        name="pair",
    )(block, swap(block, 1))

    def ring_fetch(d):
        pairs = []
        for i in range(devices):
            for c in range(4):
                place = (i + (RING - d if c % 2 else d)) % RING
                pairs.append(((RING * (i // RING) + place) * 4 + c, i * 4 + c))
        return lax.ppermute(both, ("tm", "chan"), pairs)

    came = {d: ring_fetch(d) for d in (3, 2, 1)}
    came[1], far = lax.optimization_barrier((came[1], far))
    edge = (RING - 2) * block_rows
    ring, head, tail = pl.pallas_call(
        ring_kernel,
        out_shape=tuple(jax.ShapeDtypeStruct((n, 2 * width), bf16) for n in (RING * block_rows, edge, edge)),
        in_specs=vmem(8),
        out_specs=tuple(vmem(3)),
        compiler_params=params(8),
        cost_estimate=cost(0, 8 * edge * width),
        name="ring",
    )(block, far, *[came[d] for d in (1, 2, 3)], *[swap(came[d], 1) for d in (1, 2, 3)])
    before = lax.ppermute(tail, "tm", [(i, (i + RING) % devices) for i in range(devices)])
    after = lax.ppermute(head, "tm", [((i + RING) % devices, i) for i in range(devices)])
    tap_queries, *onward = pl.pallas_call(
        tap_query_kernel,
        out_shape=tuple(jax.ShapeDtypeStruct((n, width), bf16) for n in (half, half // 2, half // 2, 2 * width)),
        in_specs=vmem(6) + [anywhere],
        out_specs=tuple(vmem(4)),
        compiler_params=params(),
        cost_estimate=cost(0, 0),
        name="tap_query",
    )(*body_pieces, query_weights, from_chip, ring)
    from_far = [swap(piece, 1) for piece in onward]

    queries = pl.pallas_call(
        query_kernel,
        out_shape=tuple(jax.ShapeDtypeStruct((n * TILE, width), bf16) for n in CHUNKS),
        in_specs=vmem(7),
        out_specs=tuple(vmem(len(CHUNKS))),
        scratch_shapes=[pltpu.VMEM((2, FRAME, width), bf16)],
        compiler_params=params(),
        cost_estimate=cost(0, 0),
        name="query",
    )(
        tap_queries,
        rest_across,
        from_core,
        from_chip,
        from_far[0],
        from_far[1],
        query_weights,
    )

    count = (2 * REACH + 1) * block_rows
    heads = width // HDIM
    starts = [sum(CHUNKS[:i]) for i in range(len(CHUNKS))]
    first = half // width
    attended = []
    came = []
    marks = []
    result = None

    def attend(i):
        chunk = CHUNKS[i] * TILE
        waited = attended[-1:] + (marks[-1:] if i == 3 else []) + (came[i - 2 : i - 1] if i >= 2 else [])
        out = pl.pallas_call(
            attend_kernel,
            out_shape=jax.ShapeDtypeStruct((chunk, width), bf16),
            in_specs=vmem(4) + [anywhere] * len(waited),
            out_specs=vmem(1)[0],
            scratch_shapes=[
                pltpu.VMEM((2 * edge + ring.shape[0], 2 * width), bf16),
                pltpu.VMEM((heads, count, width), bf16),
                pltpu.VMEM((heads, count, width), bf16),
            ],
            compiler_params=params(30),
            cost_estimate=cost(0, 0),
            name=f"attend{i}",
        )(queries[i], before, ring, after, *waited)
        attended.append(out)
        came.append(swap(out, 2))
        return out, swap(out, 1), came[-1]

    def finish(i, pieces, result):
        own, beside, across = pieces[i]
        extra = () if result is None else (result,)
        n = min(i + 2, len(CHUNKS) - 1)
        if i < n:
            onward, later = lax.optimization_barrier((across, pieces[n][0]))
            pieces[n] = (later, *pieces[n][1:])
        else:
            onward, later = lax.optimization_barrier((across, marks[i - 1]))
            extra = (*extra, later)
        start, tiles = starts[i], CHUNKS[i]
        result, mark = pl.pallas_call(
            out_kernel,
            grid=(tiles,),
            out_shape=(jax.ShapeDtypeStruct((rows, width), bf16), jax.ShapeDtypeStruct((8, 128), jnp.float32)),
            in_specs=[pl.BlockSpec((TILE, width), lambda s: (s, 0))] * 4
            + [pl.BlockSpec((width, width), lambda s, at=at: (at, 0)) for at in (0, first, first, 1)]
            + [pl.BlockSpec((TILE, width), lambda s: (start + s, 0))]
            + [anywhere] * len(extra),
            out_specs=(
                pl.BlockSpec((TILE, width), lambda s: (start + s, 0)),
                pl.BlockSpec((8, 128), lambda s: (0, 0)),
            ),
            input_output_aliases={9: 0} if extra else {},
            compiler_params=params(),
            cost_estimate=cost(0, 0),
            name=f"out{i}",
        )(own, beside, across, swap(onward, 1), w_own, from_core, from_chip, from_far[2], tokens, *extra)
        marks.append(mark)
        return result

    pieces = [attend(i) for i in range(3)]
    for i in range(len(CHUNKS)):
        result = finish(i, pieces, result)
        if i + 3 < len(CHUNKS):
            pieces.append(attend(i + 3))
    return result


def solution(mesh):
    return jax.shard_map(
        per_device,
        mesh=mesh,
        in_specs=(
            P("tm", "chan"),
            P(None, "chan"),
            P(None, "chan"),
            P(None, "chan"),
            P("chan", None),
            P(),
        ),
        out_specs=P("tm", "chan"),
        check_vma=False,
    )
```

```python
import functools
import math

import jax
import jax.numpy as jnp
import ml_dtypes
import numpy as np
from jax import lax
from jax.experimental import pallas as pl
from jax.experimental.pallas import tpu as pltpu
from jax.sharding import PartitionSpec as P

D = 1024
HDIM = 64
HH = 16
WW = 16
FRAME = HH * WW
POOL_ROWS = (HH // 4) * (WW // 4)
TAP_ROWS = FRAME // 2
RING = 8
REACH = 6
TILE = 256
CHUNKS = ((1,), (2,), (2,), (1, 2))
EPSILON = 1e-06
MB = 1024 * 1024


def tap_order():
    wanted = []
    for second in range(3):
        for third in range(3):
            for row in range(HH // 4):
                for col in range(WW // 4):
                    i, j = 4 * row - 1 + second, 4 * col - 1 + third
                    wanted.append(i * WW + j if i >= 0 and j >= 0 else -1)
    used = sorted(set(t for t in wanted if t >= 0))
    order = np.array(used + [t for t in range(FRAME) if t not in set(used)])
    place = np.argsort(order)
    return order, np.array([place[t] if t >= 0 else -1 for t in wanted])


ORDER, TAP_PLACE = tap_order()
TAP_GATHER = (TAP_PLACE[:, None] == np.arange(TAP_ROWS)[None, :]).astype(ml_dtypes.bfloat16)


def place_of(token):
    i, j = token // WW, token % WW
    rows_before, cols_before = i - (i + 1) // 4, j - (j + 1) // 4
    row_used = (i % 4 != 2) & (i != HH - 1)
    col_used = (j % 4 != 2) & (j != WW - 1)
    side = HH - 1 - HH // 4
    used_before = rows_before * side + jnp.where(row_used, cols_before, 0)
    return jnp.where(row_used & col_used, used_before, side * side + token - used_before)


def move_matrix(back):
    token = lax.broadcasted_iota(jnp.int32, (FRAME, 1) if back else (1, FRAME), 0 if back else 1)
    place = lax.broadcasted_iota(jnp.int32, (FRAME, FRAME), 1 if back else 0)
    return jnp.where(place_of(token) == place, 1.0, 0.0).astype(jnp.bfloat16)


def vmem(count):
    return [pl.BlockSpec(memory_space=pltpu.VMEM)] * count


def params(limit=20):
    return pltpu.CompilerParams(vmem_limit_bytes=limit * MB)


def cost(flops, moved, exps=0):
    return pl.CostEstimate(flops=int(flops), bytes_accessed=int(moved), transcendentals=int(exps))


def dot(a, b):
    return jnp.dot(a, b, preferred_element_type=jnp.float32)


def arrange_kernel(
    tokens_hbm, w_out_hbm, taps_ref, last_ref, across_ref, beside_ref, own_ref, tokens_ref, w_out_ref, frame_sems, w_sem
):
    me = lax.axis_index("chan")
    frames = tokens_ref.shape[0] // FRAME
    count = frames * TAP_ROWS
    width = w_out_ref.shape[0]
    order = [frames - 1] + list(range(frames - 1))

    def frame_copy(f):
        rows = pl.ds(f * FRAME, FRAME)
        return pltpu.make_async_copy(tokens_hbm.at[rows, :], tokens_ref.at[rows, :], frame_sems.at[f])

    for f in order:
        frame_copy(f).start()
    w_copy = pltpu.make_async_copy(w_out_hbm, w_out_ref, w_sem)
    w_copy.start()
    gather = move_matrix(False)
    for f in order:
        frame_copy(f).wait()
        moved = dot(gather, tokens_ref[f * FRAME : (f + 1) * FRAME, :]).astype(jnp.bfloat16)
        taps_ref[f * TAP_ROWS : (f + 1) * TAP_ROWS, :] = moved[:TAP_ROWS]
        if f == frames - 1:
            last_ref[...] = moved[:TAP_ROWS]
        across_ref[f * TAP_ROWS : (f + 1) * TAP_ROWS, :] = moved[TAP_ROWS:]
        beside_ref[f * TAP_ROWS : (f + 1) * TAP_ROWS, :] = moved[TAP_ROWS:]
    w_copy.wait()

    def columns(k):
        return w_out_ref[:, pl.ds(pl.multiple_of((me ^ k) * width, width), width)]

    own_ref[...] = columns(0)
    beside_ref[count:, :] = columns(1)
    across_ref[count : count + width, :] = columns(2)
    across_ref[count + width :, :] = columns(3)


def pack_kernel(wk_hbm, wv_hbm, wq_hbm, pool_ref, key_value_ref, query_ref, taps_ref, sems):
    me = lax.axis_index("chan")
    width = query_ref.shape[1]
    copies = []
    for k in range(4):
        source = pl.ds(pl.multiple_of((me ^ k) * width, width), width)
        target = pl.ds(k * width, width)
        copies += [
            pltpu.make_async_copy(
                wk_hbm.at[source, :], key_value_ref.at[target, pl.ds(0, width)], sems.at[3 * k]
            ),
            pltpu.make_async_copy(
                wv_hbm.at[source, :], key_value_ref.at[target, pl.ds(width, width)], sems.at[3 * k + 1]
            ),
            pltpu.make_async_copy(wq_hbm.at[source, :], query_ref.at[target, :], sems.at[3 * k + 2]),
        ]
    for copy in copies:
        copy.start()
    heads = width // HDIM
    taps_ref[...] = jnp.concatenate([pool_ref[0]] * heads + [pool_ref[1]] * heads, axis=1)
    for copy in copies:
        copy.wait()


def project(pieces, start, count, weights):
    rows = jnp.concatenate([piece[start : start + count, :] for piece in pieces], axis=1)
    return dot(rows, weights).astype(jnp.bfloat16)


def weigh(slabs, taps, first):
    total = None
    for q in range(9):
        term = slabs[q * POOL_ROWS : (q + 1) * POOL_ROWS] * taps[9 * first + q : 9 * first + q + 1, :]
        total = term if total is None else total + term
    return total


def group_mean(rows, averaging):
    high = rows.astype(jnp.bfloat16)
    rest = rows - high.astype(jnp.float32)
    middle = rest.astype(jnp.bfloat16)
    low = (rest - middle.astype(jnp.float32)).astype(jnp.bfloat16)
    return dot(high, averaging) + dot(middle, averaging) + dot(low, averaging)


def pool_kernel_body(a0, a1, a2, a3, l0, l1, l2, l3, weights_ref, taps_ref, spread_ref, out_ref):
    width = weights_ref.shape[1] // 2
    lane = lax.broadcasted_iota(jnp.int32, (width, width), 1) // HDIM
    row = lax.broadcasted_iota(jnp.int32, (width, width), 0) // HDIM
    averaging = jnp.where(lane == row, 1.0 / HDIM, 0.0).astype(jnp.bfloat16)
    frames = a0.shape[0] // TAP_ROWS
    pooled_frames = frames // 2
    weights = weights_ref[...]
    taps = taps_ref[...]
    spread = spread_ref[...]
    sums = [None] * pooled_frames
    sums[0] = weigh(dot(spread, project((l0, l1, l2, l3), 0, TAP_ROWS, weights)), taps, 0)
    for f in range(frames):
        slabs = dot(spread, project((a0, a1, a2, a3), f * TAP_ROWS, TAP_ROWS, weights))
        t = f // 2
        part = weigh(slabs, taps, 1 + f % 2)
        sums[t] = part if sums[t] is None else sums[t] + part
        if f % 2 == 1 and t + 1 < pooled_frames:
            sums[t + 1] = weigh(slabs, taps, 0)
    pooled = jnp.concatenate(sums, axis=0)
    for side in range(2):
        lanes = slice(side * width, (side + 1) * width)
        center = pooled[:, lanes] - group_mean(pooled[:, lanes], averaging)
        spread_rows = group_mean(center * center, averaging)
        normal = (center * lax.rsqrt(spread_rows + EPSILON)).astype(jnp.bfloat16)
        out_ref[:, lanes] = normal


def tap_query_kernel(a0, a1, a2, a3, wq_ref, came_ref, after_ref, q_ref, *parts):
    del after_ref
    step = 2 * FRAME
    for start in range(0, q_ref.shape[0], step):
        q_ref[start : start + step, :] = project((a0, a1, a2, a3), start, step, wq_ref[...])
    at = 0
    for part in parts:
        part[...] = came_ref[at : at + part.shape[0], :]
        at += part.shape[0]


def query_kernel(q_ref, b0, b1, b2, c0, c1, wq_ref, *rest):
    outs, both = rest[:-1], rest[-1]
    frames = q_ref.shape[0] // TAP_ROWS
    back = move_matrix(True)
    places = [(ref, start) for ref in outs for start in range(0, ref.shape[0], FRAME)]
    far = c0.shape[0]
    for f in range(frames):
        at = f * TAP_ROWS
        both[f % 2, :TAP_ROWS, :] = q_ref[at : at + TAP_ROWS, :]
        c = c0 if at < far else c1
        pieces = [piece[at : at + TAP_ROWS, :] for piece in (b0, b1, b2)] + [c[at % far : at % far + TAP_ROWS, :]]
        others = dot(jnp.concatenate(pieces, axis=1), wq_ref[...])
        both[f % 2, TAP_ROWS:, :] = others.astype(jnp.bfloat16)
        ref, start = places[f]
        ref[start : start + FRAME, :] = dot(back, both[f % 2]).astype(jnp.bfloat16)


def pair_kernel(own_ref, peer_ref, both_ref):
    block = own_ref.shape[0]
    both_ref[:block, :] = own_ref[...]
    both_ref[block:, :] = peer_ref[...]


def ring_kernel(own, far, r1, r2, r3, s1, s2, s3, ring_ref, head_ref, tail_ref):
    z = lax.rem(lax.axis_index("tm"), RING)
    core = lax.rem(lax.axis_index("chan"), 2)
    block = own.shape[0]
    edge = head_ref.shape[0]

    def put(place, value):
        ring_ref[pl.ds(pl.multiple_of(lax.rem(place, RING) * block, block), block), :] = value

    put(z, own[...])
    put(z + RING // 2, far[...])
    for d, r, s in ((1, r1, s1), (2, r2, s2), (3, r3, s3)):
        step = d + core * (RING - 2 * d)
        put(z + step, r[:block, :])
        put(z + RING - step, s[block:, :])
    head_ref[...] = ring_ref[:edge, :]
    tail_ref[...] = ring_ref[ring_ref.shape[0] - edge :, :]


def attend_kernel(parts, q_ref, before_ref, here_ref, after_ref, *rest):
    outs, (window, keys, values) = rest[-3 - parts : -3], rest[-3:]
    width = q_ref.shape[1]
    heads = width // HDIM
    block = here_ref.shape[0] // RING
    count = keys.shape[1]
    z = lax.rem(lax.axis_index("tm"), RING)

    n = before_ref.shape[0]
    m = here_ref.shape[0]
    window[:n, :] = before_ref[...]
    window[n : n + m, :] = here_ref[...]
    window[n + m :, :] = after_ref[...]
    rows = window[pl.ds(pl.multiple_of(z * block, block), count), :]
    head = lax.broadcasted_iota(jnp.int32, (count, width), 1) // HDIM
    k = rows[:, :width].astype(jnp.float32) * (1.0 / math.sqrt(HDIM))
    v = rows[:, width:].astype(jnp.float32)
    for h in range(heads):
        keys[h] = jnp.where(head == h, k, 0.0).astype(jnp.bfloat16)
        values[h] = jnp.where(head == h, v, 0.0).astype(jnp.bfloat16)

    q = q_ref[...]
    total = q.astype(jnp.float32)
    for h in range(heads):
        scores = lax.dot_general(q, keys[h], (((1,), (1,)), ((), ())), preferred_element_type=jnp.float32)
        top = jnp.max(scores, axis=-1, keepdims=True)
        weighted = jnp.exp(scores - top)
        summed = jnp.sum(weighted, axis=-1, keepdims=True)
        total = total + dot(weighted.astype(jnp.bfloat16), values[h]) * (1.0 / summed)
    at = 0
    for ref in outs:
        ref[...] = total[at : at + ref.shape[0]].astype(jnp.bfloat16)
        at += ref.shape[0]


def out_kernel(a0, a1, a2, a3, w0, w1, w2, w3, tokens_ref, *rest):
    out_ref, done_ref = rest[-2:]
    done_ref[...] = jnp.zeros_like(done_ref)
    total = tokens_ref[...].astype(jnp.float32)
    acc = dot(a0[...], w0[...])
    for a, w in ((a1, w1), (a2, w2), (a3, w3)):
        acc = acc + dot(a[...], w[...])
    out_ref[...] = (total + acc).astype(jnp.bfloat16)


def swap(array, k):
    return lax.ppermute(array, "chan", [(i, i ^ k) for i in range(4)])


def per_device(tokens, w_query, w_key, w_value, w_out, pool_kernel):
    rows, width = tokens.shape
    frames = rows // FRAME
    devices = lax.axis_size("tm")
    bf16 = jnp.bfloat16
    tap_gather = jnp.asarray(TAP_GATHER)
    anywhere = pl.BlockSpec(memory_space=pl.ANY)

    hbm = pl.BlockSpec(memory_space=pltpu.HBM)
    half = frames * TAP_ROWS
    body, last, rest_across, rest_beside, w_own = pl.pallas_call(
        arrange_kernel,
        out_shape=(
            jax.ShapeDtypeStruct((half, width), bf16),
            jax.ShapeDtypeStruct((TAP_ROWS, width), bf16),
            jax.ShapeDtypeStruct((half + 2 * width, width), bf16),
            jax.ShapeDtypeStruct((half + width, width), bf16),
            jax.ShapeDtypeStruct((width, width), bf16),
        ),
        in_specs=[hbm] * 2,
        out_specs=tuple(vmem(5)),
        scratch_shapes=[
            pltpu.VMEM((rows, width), bf16),
            pltpu.VMEM((width, D), bf16),
            pltpu.SemaphoreType.DMA((frames,)),
            pltpu.SemaphoreType.DMA,
        ],
        compiler_params=params(60),
        cost_estimate=cost(2 * rows * FRAME * width, 4 * rows * width),
        name="arrange",
    )(tokens, w_out)
    key_value_weights, query_weights, taps = pl.pallas_call(
        pack_kernel,
        out_shape=(
            jax.ShapeDtypeStruct((D, 2 * width), bf16),
            jax.ShapeDtypeStruct((D, width), bf16),
            jax.ShapeDtypeStruct((pool_kernel.shape[1], 2 * width), jnp.float32),
        ),
        in_specs=[hbm] * 3 + vmem(1),
        out_specs=tuple(vmem(3)),
        scratch_shapes=[pltpu.SemaphoreType.DMA((12,))],
        compiler_params=params(8),
        cost_estimate=cost(0, 12 * D * width),
        name="pack",
    )(w_key, w_value, w_query, pool_kernel)
    last = lax.ppermute(last, "tm", [(i, (i + 1) % devices) for i in range(devices)])

    last, key_value_weights = lax.optimization_barrier((last, key_value_weights))
    last_across = swap(last, 2)
    body_across, last_across = lax.optimization_barrier((swap(body, 2), last_across))
    body_pieces = (body, swap(body, 1), body_across, swap(body_across, 1))
    last_pieces = (last, swap(last, 1), last_across, swap(last_across, 1))
    rest_later, last_came = lax.optimization_barrier((rest_across, last_pieces[2]))
    last_pieces = (*last_pieces[:2], last_came, last_pieces[3])
    from_chip = swap(rest_later, 2)
    from_core = swap(rest_beside, 1)

    block = pl.pallas_call(
        pool_kernel_body,
        out_shape=jax.ShapeDtypeStruct((frames // 2 * POOL_ROWS, 2 * width), bf16),
        in_specs=vmem(11),
        out_specs=vmem(1)[0],
        compiler_params=params(),
        cost_estimate=cost(2 * frames * TAP_ROWS * D * 2 * width, 8 * rows * width),
        name="pool",
    )(*body_pieces, *last_pieces, key_value_weights, taps, tap_gather)

    block_rows = block.shape[0]
    far = lax.ppermute(
        block, "tm", [(RING * (i // RING) + (i + RING // 2) % RING, i) for i in range(devices)]
    )
    both = pl.pallas_call(
        pair_kernel,
        out_shape=jax.ShapeDtypeStruct((2 * block_rows, 2 * width), bf16),
        in_specs=vmem(2),
        out_specs=vmem(1)[0],
        compiler_params=params(4),
        cost_estimate=cost(0, 0),
        name="pair",
    )(block, swap(block, 1))

    def ring_fetch(d):
        pairs = []
        for i in range(devices):
            for c in range(4):
                place = (i + (RING - d if c % 2 else d)) % RING
                pairs.append(((RING * (i // RING) + place) * 4 + c, i * 4 + c))
        return lax.ppermute(both, ("tm", "chan"), pairs)

    came = {d: ring_fetch(d) for d in (3, 2, 1)}
    came[1], far = lax.optimization_barrier((came[1], far))
    edge = (RING - 2) * block_rows
    ring, head, tail = pl.pallas_call(
        ring_kernel,
        out_shape=tuple(jax.ShapeDtypeStruct((n, 2 * width), bf16) for n in (RING * block_rows, edge, edge)),
        in_specs=vmem(8),
        out_specs=tuple(vmem(3)),
        compiler_params=params(8),
        cost_estimate=cost(0, 8 * edge * width),
        name="ring",
    )(block, far, *[came[d] for d in (1, 2, 3)], *[swap(came[d], 1) for d in (1, 2, 3)])
    before = lax.ppermute(tail, "tm", [(i, (i + RING) % devices) for i in range(devices)])
    after = lax.ppermute(head, "tm", [((i + RING) % devices, i) for i in range(devices)])
    tap_queries, *onward = pl.pallas_call(
        tap_query_kernel,
        out_shape=tuple(jax.ShapeDtypeStruct((n, width), bf16) for n in (half, half // 2, half // 2, 2 * width)),
        in_specs=vmem(6) + [anywhere],
        out_specs=tuple(vmem(4)),
        compiler_params=params(),
        cost_estimate=cost(0, 0),
        name="tap_query",
    )(*body_pieces, query_weights, from_chip, ring)
    from_far = [swap(piece, 1) for piece in onward]

    queries = pl.pallas_call(
        query_kernel,
        out_shape=tuple(jax.ShapeDtypeStruct((sum(parts) * TILE, width), bf16) for parts in CHUNKS),
        in_specs=vmem(7),
        out_specs=tuple(vmem(len(CHUNKS))),
        scratch_shapes=[pltpu.VMEM((2, FRAME, width), bf16)],
        compiler_params=params(),
        cost_estimate=cost(0, 0),
        name="query",
    )(
        tap_queries,
        rest_across,
        from_core,
        from_chip,
        from_far[0],
        from_far[1],
        query_weights,
    )

    count = (2 * REACH + 1) * block_rows
    heads = width // HDIM
    sends = [tiles for parts in CHUNKS for tiles in parts]
    starts = [sum(sends[:i]) for i in range(len(sends))]
    first = half // width
    pieces = []
    came = []
    marks = []
    result = None

    def attend(i, parts, query):
        waited = [pieces[-1][0]] if pieces else []
        waited += marks[:1] if i == 3 else []
        waited += came[i - 2 : i - 1] if i >= 2 else []
        outs = pl.pallas_call(
            functools.partial(attend_kernel, len(parts)),
            out_shape=tuple(jax.ShapeDtypeStruct((tiles * TILE, width), bf16) for tiles in parts),
            in_specs=vmem(4) + [anywhere] * len(waited),
            out_specs=tuple(vmem(len(parts))),
            scratch_shapes=[
                pltpu.VMEM((2 * edge + ring.shape[0], 2 * width), bf16),
                pltpu.VMEM((heads, count, width), bf16),
                pltpu.VMEM((heads, count, width), bf16),
            ],
            compiler_params=params(30),
            cost_estimate=cost(0, 0),
            name=f"attend{i}",
        )(query, before, ring, after, *waited)
        for out in outs:
            came.append(swap(out, 2))
            pieces.append((out, swap(out, 1), came[-1]))

    def finish(i, result):
        own, beside, across = pieces[i]
        extra = () if result is None else (result,)
        n = min(i + 2, 3)
        if i < n:
            onward, later = lax.optimization_barrier((across, pieces[n][0]))
            pieces[n] = (later, *pieces[n][1:])
        else:
            onward, later = lax.optimization_barrier((across, marks[i - 1 if i == 4 else 1]))
            extra = (*extra, later)
        start, tiles = starts[i], sends[i]
        result, mark = pl.pallas_call(
            out_kernel,
            grid=(tiles,),
            out_shape=(jax.ShapeDtypeStruct((rows, width), bf16), jax.ShapeDtypeStruct((8, 128), jnp.float32)),
            in_specs=[pl.BlockSpec((TILE, width), lambda s: (s, 0))] * 4
            + [pl.BlockSpec((width, width), lambda s, at=at: (at, 0)) for at in (0, first, first, 1)]
            + [pl.BlockSpec((TILE, width), lambda s: (start + s, 0))]
            + [anywhere] * len(extra),
            out_specs=(
                pl.BlockSpec((TILE, width), lambda s: (start + s, 0)),
                pl.BlockSpec((8, 128), lambda s: (0, 0)),
            ),
            input_output_aliases={9: 0} if extra else {},
            compiler_params=params(),
            cost_estimate=cost(0, 0),
            name=f"out{i}",
        )(own, beside, across, swap(onward, 1), w_own, from_core, from_chip, from_far[2], tokens, *extra)
        marks.append(mark)
        return result

    for i in range(3):
        attend(i, CHUNKS[i], queries[i])
    result = finish(0, result)
    attend(3, CHUNKS[3], queries[3])
    for i in range(1, len(sends)):
        result = finish(i, result)
    return result


def solution(mesh):
    return jax.shard_map(
        per_device,
        mesh=mesh,
        in_specs=(
            P("tm", "chan"),
            P(None, "chan"),
            P(None, "chan"),
            P(None, "chan"),
            P("chan", None),
            P(),
        ),
        out_specs=P("tm", "chan"),
        check_vma=False,
    )
```

```python
import functools
import math

import jax
import jax.numpy as jnp
import ml_dtypes
import numpy as np
from jax import lax
from jax.experimental import pallas as pl
from jax.experimental.pallas import tpu as pltpu
from jax.sharding import PartitionSpec as P

D = 1024
HDIM = 64
HH = 16
WW = 16
FRAME = HH * WW
POOL_ROWS = (HH // 4) * (WW // 4)
TAP_ROWS = FRAME // 2
RING = 8
REACH = 6
TILE = 256
CHUNKS = ((1,), (2,), (2,), (1, 2))
EPSILON = 1e-06
MB = 1024 * 1024


def tap_order():
    wanted = []
    for second in range(3):
        for third in range(3):
            for row in range(HH // 4):
                for col in range(WW // 4):
                    i, j = 4 * row - 1 + second, 4 * col - 1 + third
                    wanted.append(i * WW + j if i >= 0 and j >= 0 else -1)
    used = sorted(set(t for t in wanted if t >= 0))
    order = np.array(used + [t for t in range(FRAME) if t not in set(used)])
    place = np.argsort(order)
    return order, np.array([place[t] if t >= 0 else -1 for t in wanted])


ORDER, TAP_PLACE = tap_order()
TAP_GATHER = (TAP_PLACE[:, None] == np.arange(TAP_ROWS)[None, :]).astype(ml_dtypes.bfloat16)


def place_of(token):
    i, j = token // WW, token % WW
    rows_before, cols_before = i - (i + 1) // 4, j - (j + 1) // 4
    row_used = (i % 4 != 2) & (i != HH - 1)
    col_used = (j % 4 != 2) & (j != WW - 1)
    side = HH - 1 - HH // 4
    used_before = rows_before * side + jnp.where(row_used, cols_before, 0)
    return jnp.where(row_used & col_used, used_before, side * side + token - used_before)


def move_matrix(back):
    token = lax.broadcasted_iota(jnp.int32, (FRAME, 1) if back else (1, FRAME), 0 if back else 1)
    place = lax.broadcasted_iota(jnp.int32, (FRAME, FRAME), 1 if back else 0)
    return jnp.where(place_of(token) == place, 1.0, 0.0).astype(jnp.bfloat16)


def vmem(count):
    return [pl.BlockSpec(memory_space=pltpu.VMEM)] * count


def params(limit=20):
    return pltpu.CompilerParams(vmem_limit_bytes=limit * MB)


def cost(flops, moved, exps=0):
    return pl.CostEstimate(flops=int(flops), bytes_accessed=int(moved), transcendentals=int(exps))


def dot(a, b):
    return jnp.dot(a, b, preferred_element_type=jnp.float32)


def arrange_kernel(
    tokens_hbm, w_out_hbm, taps_ref, last_ref, across_ref, beside_ref, own_ref, tokens_ref, w_out_ref, frame_sems, w_sem
):
    me = lax.axis_index("chan")
    frames = tokens_ref.shape[0] // FRAME
    count = frames * TAP_ROWS
    width = w_out_ref.shape[0]
    order = [frames - 1] + list(range(frames - 1))

    def frame_copy(f):
        rows = pl.ds(f * FRAME, FRAME)
        return pltpu.make_async_copy(tokens_hbm.at[rows, :], tokens_ref.at[rows, :], frame_sems.at[f])

    for f in order:
        frame_copy(f).start()
    w_copy = pltpu.make_async_copy(w_out_hbm, w_out_ref, w_sem)
    w_copy.start()
    gather = move_matrix(False)
    for f in order:
        frame_copy(f).wait()
        moved = dot(gather, tokens_ref[f * FRAME : (f + 1) * FRAME, :]).astype(jnp.bfloat16)
        taps_ref[f * TAP_ROWS : (f + 1) * TAP_ROWS, :] = moved[:TAP_ROWS]
        if f == frames - 1:
            last_ref[...] = moved[:TAP_ROWS]
        across_ref[f * TAP_ROWS : (f + 1) * TAP_ROWS, :] = moved[TAP_ROWS:]
        beside_ref[f * TAP_ROWS : (f + 1) * TAP_ROWS, :] = moved[TAP_ROWS:]
    w_copy.wait()

    def columns(k):
        return w_out_ref[:, pl.ds(pl.multiple_of((me ^ k) * width, width), width)]

    own_ref[...] = columns(0)
    beside_ref[count:, :] = columns(1)
    across_ref[count : count + width, :] = columns(2)
    across_ref[count + width :, :] = columns(3)


def pack_kernel(wk_hbm, wv_hbm, wq_hbm, pool_ref, key_value_ref, query_ref, taps_ref, sems):
    me = lax.axis_index("chan")
    width = query_ref.shape[1]
    copies = []
    for k in range(4):
        source = pl.ds(pl.multiple_of((me ^ k) * width, width), width)
        target = pl.ds(k * width, width)
        copies += [
            pltpu.make_async_copy(
                wk_hbm.at[source, :], key_value_ref.at[target, pl.ds(0, width)], sems.at[3 * k]
            ),
            pltpu.make_async_copy(
                wv_hbm.at[source, :], key_value_ref.at[target, pl.ds(width, width)], sems.at[3 * k + 1]
            ),
            pltpu.make_async_copy(wq_hbm.at[source, :], query_ref.at[target, :], sems.at[3 * k + 2]),
        ]
    for copy in copies:
        copy.start()
    heads = width // HDIM
    taps_ref[...] = jnp.concatenate([pool_ref[0]] * heads + [pool_ref[1]] * heads, axis=1)
    for copy in copies:
        copy.wait()


def project(pieces, start, count, weights):
    rows = jnp.concatenate([piece[start : start + count, :] for piece in pieces], axis=1)
    return dot(rows, weights).astype(jnp.bfloat16)


def weigh(slabs, taps, first):
    total = None
    for q in range(9):
        term = slabs[q * POOL_ROWS : (q + 1) * POOL_ROWS] * taps[9 * first + q : 9 * first + q + 1, :]
        total = term if total is None else total + term
    return total


def group_mean(rows, averaging):
    high = rows.astype(jnp.bfloat16)
    rest = rows - high.astype(jnp.float32)
    middle = rest.astype(jnp.bfloat16)
    low = (rest - middle.astype(jnp.float32)).astype(jnp.bfloat16)
    return dot(high, averaging) + dot(middle, averaging) + dot(low, averaging)


def pool_kernel_body(a0, a1, a2, a3, l0, l1, l2, l3, weights_ref, taps_ref, spread_ref, out_ref, twice_ref):
    width = weights_ref.shape[1] // 2
    lane = lax.broadcasted_iota(jnp.int32, (width, width), 1) // HDIM
    row = lax.broadcasted_iota(jnp.int32, (width, width), 0) // HDIM
    averaging = jnp.where(lane == row, 1.0 / HDIM, 0.0).astype(jnp.bfloat16)
    frames = a0.shape[0] // TAP_ROWS
    pooled_frames = frames // 2
    weights = weights_ref[...]
    taps = taps_ref[...]
    spread = spread_ref[...]
    sums = [None] * pooled_frames
    sums[0] = weigh(dot(spread, project((l0, l1, l2, l3), 0, TAP_ROWS, weights)), taps, 0)
    for f in range(frames):
        slabs = dot(spread, project((a0, a1, a2, a3), f * TAP_ROWS, TAP_ROWS, weights))
        t = f // 2
        part = weigh(slabs, taps, 1 + f % 2)
        sums[t] = part if sums[t] is None else sums[t] + part
        if f % 2 == 1 and t + 1 < pooled_frames:
            sums[t + 1] = weigh(slabs, taps, 0)
    pooled = jnp.concatenate(sums, axis=0)
    for side in range(2):
        lanes = slice(side * width, (side + 1) * width)
        center = pooled[:, lanes] - group_mean(pooled[:, lanes], averaging)
        spread_rows = group_mean(center * center, averaging)
        normal = (center * lax.rsqrt(spread_rows + EPSILON)).astype(jnp.bfloat16)
        out_ref[:, lanes] = normal
        for copy in range(twice_ref.shape[0]):
            twice_ref[copy, :, lanes] = normal


def tap_query_kernel(a0, a1, a2, a3, wq_ref, came_ref, after_ref, q_ref, *parts):
    del after_ref
    step = 2 * FRAME
    for start in range(0, q_ref.shape[0], step):
        q_ref[start : start + step, :] = project((a0, a1, a2, a3), start, step, wq_ref[...])
    at = 0
    for part in parts:
        part[...] = came_ref[at : at + part.shape[0], :]
        at += part.shape[0]


def query_kernel(q_ref, b0, b1, b2, c0, c1, wq_ref, *rest):
    outs, both = rest[:-1], rest[-1]
    frames = q_ref.shape[0] // TAP_ROWS
    back = move_matrix(True)
    places = [(ref, start) for ref in outs for start in range(0, ref.shape[0], FRAME)]
    far = c0.shape[0]
    for f in range(frames):
        at = f * TAP_ROWS
        both[f % 2, :TAP_ROWS, :] = q_ref[at : at + TAP_ROWS, :]
        c = c0 if at < far else c1
        pieces = [piece[at : at + TAP_ROWS, :] for piece in (b0, b1, b2)] + [c[at % far : at % far + TAP_ROWS, :]]
        others = dot(jnp.concatenate(pieces, axis=1), wq_ref[...])
        both[f % 2, TAP_ROWS:, :] = others.astype(jnp.bfloat16)
        ref, start = places[f]
        ref[start : start + FRAME, :] = dot(back, both[f % 2]).astype(jnp.bfloat16)


def pair_kernel(own_ref, peer_ref, both_ref):
    block = own_ref.shape[0]
    both_ref[:block, :] = own_ref[...]
    both_ref[block:, :] = peer_ref[...]


def ring_kernel(opposite, r1, r2, r3, s1, s2, s3, ring_ref, head_ref, tail_ref):
    z = lax.rem(lax.axis_index("tm"), RING)
    core = lax.rem(lax.axis_index("chan"), 2)
    block = opposite.shape[1]
    edge = head_ref.shape[0]

    def put(place, value):
        ring_ref[pl.ds(pl.multiple_of(lax.rem(place, RING) * block, block), block), :] = value

    for member in range(2):
        put(lax.rem(z, RING // 2) + member * (RING // 2), opposite[member])
    for d, r, s in ((1, r1, s1), (2, r2, s2), (3, r3, s3)):
        step = d + core * (RING - 2 * d)
        put(z + step, r[:block, :])
        put(z + RING - step, s[block:, :])
    head_ref[...] = ring_ref[:edge, :]
    tail_ref[...] = ring_ref[ring_ref.shape[0] - edge :, :]


def attend_kernel(parts, q_ref, before_ref, here_ref, after_ref, *rest):
    outs, (window, keys, values) = rest[-3 - parts : -3], rest[-3:]
    width = q_ref.shape[1]
    heads = width // HDIM
    block = here_ref.shape[0] // RING
    count = keys.shape[1]
    z = lax.rem(lax.axis_index("tm"), RING)

    n = before_ref.shape[0]
    m = here_ref.shape[0]
    window[:n, :] = before_ref[...]
    window[n : n + m, :] = here_ref[...]
    window[n + m :, :] = after_ref[...]
    rows = window[pl.ds(pl.multiple_of(z * block, block), count), :]
    head = lax.broadcasted_iota(jnp.int32, (count, width), 1) // HDIM
    k = rows[:, :width].astype(jnp.float32) * (1.0 / math.sqrt(HDIM))
    v = rows[:, width:].astype(jnp.float32)
    for h in range(heads):
        keys[h] = jnp.where(head == h, k, 0.0).astype(jnp.bfloat16)
        values[h] = jnp.where(head == h, v, 0.0).astype(jnp.bfloat16)

    q = q_ref[...]
    total = q.astype(jnp.float32)
    for h in range(heads):
        scores = lax.dot_general(q, keys[h], (((1,), (1,)), ((), ())), preferred_element_type=jnp.float32)
        top = jnp.max(scores, axis=-1, keepdims=True)
        weighted = jnp.exp(scores - top)
        summed = jnp.sum(weighted, axis=-1, keepdims=True)
        total = total + dot(weighted.astype(jnp.bfloat16), values[h]) * (1.0 / summed)
    at = 0
    for ref in outs:
        ref[...] = total[at : at + ref.shape[0]].astype(jnp.bfloat16)
        at += ref.shape[0]


def out_kernel(a0, a1, a2, a3, w0, w1, w2, w3, tokens_ref, *rest):
    out_ref, done_ref = rest[-2:]
    done_ref[...] = jnp.zeros_like(done_ref)
    total = tokens_ref[...].astype(jnp.float32)
    acc = dot(a0[...], w0[...])
    for a, w in ((a1, w1), (a2, w2), (a3, w3)):
        acc = acc + dot(a[...], w[...])
    out_ref[...] = (total + acc).astype(jnp.bfloat16)


def swap(array, k):
    return lax.ppermute(array, "chan", [(i, i ^ k) for i in range(4)])


def per_device(tokens, w_query, w_key, w_value, w_out, pool_kernel):
    rows, width = tokens.shape
    frames = rows // FRAME
    devices = lax.axis_size("tm")
    bf16 = jnp.bfloat16
    tap_gather = jnp.asarray(TAP_GATHER)
    anywhere = pl.BlockSpec(memory_space=pl.ANY)

    hbm = pl.BlockSpec(memory_space=pltpu.HBM)
    half = frames * TAP_ROWS
    body, last, rest_across, rest_beside, w_own = pl.pallas_call(
        arrange_kernel,
        out_shape=(
            jax.ShapeDtypeStruct((half, width), bf16),
            jax.ShapeDtypeStruct((TAP_ROWS, width), bf16),
            jax.ShapeDtypeStruct((half + 2 * width, width), bf16),
            jax.ShapeDtypeStruct((half + width, width), bf16),
            jax.ShapeDtypeStruct((width, width), bf16),
        ),
        in_specs=[hbm] * 2,
        out_specs=tuple(vmem(5)),
        scratch_shapes=[
            pltpu.VMEM((rows, width), bf16),
            pltpu.VMEM((width, D), bf16),
            pltpu.SemaphoreType.DMA((frames,)),
            pltpu.SemaphoreType.DMA,
        ],
        compiler_params=params(60),
        cost_estimate=cost(2 * rows * FRAME * width, 4 * rows * width),
        name="arrange",
    )(tokens, w_out)
    key_value_weights, query_weights, taps = pl.pallas_call(
        pack_kernel,
        out_shape=(
            jax.ShapeDtypeStruct((D, 2 * width), bf16),
            jax.ShapeDtypeStruct((D, width), bf16),
            jax.ShapeDtypeStruct((pool_kernel.shape[1], 2 * width), jnp.float32),
        ),
        in_specs=[hbm] * 3 + vmem(1),
        out_specs=tuple(vmem(3)),
        scratch_shapes=[pltpu.SemaphoreType.DMA((12,))],
        compiler_params=params(8),
        cost_estimate=cost(0, 12 * D * width),
        name="pack",
    )(w_key, w_value, w_query, pool_kernel)
    last = lax.ppermute(last, "tm", [(i, (i + 1) % devices) for i in range(devices)])

    last, key_value_weights = lax.optimization_barrier((last, key_value_weights))
    last_across = swap(last, 2)
    body_across, last_across = lax.optimization_barrier((swap(body, 2), last_across))
    body_pieces = (body, swap(body, 1), body_across, swap(body_across, 1))
    last_pieces = (last, swap(last, 1), last_across, swap(last_across, 1))
    rest_later, last_came = lax.optimization_barrier((rest_across, last_pieces[2]))
    last_pieces = (*last_pieces[:2], last_came, last_pieces[3])
    from_chip = swap(rest_later, 2)
    from_core = swap(rest_beside, 1)

    block, twice = pl.pallas_call(
        pool_kernel_body,
        out_shape=(
            jax.ShapeDtypeStruct((frames // 2 * POOL_ROWS, 2 * width), bf16),
            jax.ShapeDtypeStruct((2, frames // 2 * POOL_ROWS, 2 * width), bf16),
        ),
        in_specs=vmem(11),
        out_specs=tuple(vmem(2)),
        compiler_params=params(),
        cost_estimate=cost(2 * frames * TAP_ROWS * D * 2 * width, 8 * rows * width),
        name="pool",
    )(*body_pieces, *last_pieces, key_value_weights, taps, tap_gather)

    block_rows = block.shape[0]
    across_ring = [[RING * r + q, RING * r + q + RING // 2] for r in range(devices // RING) for q in range(RING // 2)]
    opposite = lax.all_to_all(twice, "tm", 0, 0, axis_index_groups=across_ring)
    both = pl.pallas_call(
        pair_kernel,
        out_shape=jax.ShapeDtypeStruct((2 * block_rows, 2 * width), bf16),
        in_specs=vmem(2),
        out_specs=vmem(1)[0],
        compiler_params=params(4),
        cost_estimate=cost(0, 0),
        name="pair",
    )(block, swap(block, 1))

    def ring_fetch(d):
        pairs = []
        for i in range(devices):
            for c in range(4):
                place = (i + (RING - d if c % 2 else d)) % RING
                pairs.append(((RING * (i // RING) + place) * 4 + c, i * 4 + c))
        return lax.ppermute(both, ("tm", "chan"), pairs)

    came = {d: ring_fetch(d) for d in (3, 2, 1)}
    came[1], opposite = lax.optimization_barrier((came[1], opposite))
    edge = (RING - 2) * block_rows
    ring, head, tail = pl.pallas_call(
        ring_kernel,
        out_shape=tuple(jax.ShapeDtypeStruct((n, 2 * width), bf16) for n in (RING * block_rows, edge, edge)),
        in_specs=vmem(7),
        out_specs=tuple(vmem(3)),
        compiler_params=params(8),
        cost_estimate=cost(0, 8 * edge * width),
        name="ring",
    )(opposite, *[came[d] for d in (1, 2, 3)], *[swap(came[d], 1) for d in (1, 2, 3)])
    before = lax.ppermute(tail, "tm", [(i, (i + RING) % devices) for i in range(devices)])
    after = lax.ppermute(head, "tm", [((i + RING) % devices, i) for i in range(devices)])
    tap_queries, *onward = pl.pallas_call(
        tap_query_kernel,
        out_shape=tuple(jax.ShapeDtypeStruct((n, width), bf16) for n in (half, half // 2, half // 2, 2 * width)),
        in_specs=vmem(6) + [anywhere],
        out_specs=tuple(vmem(4)),
        compiler_params=params(),
        cost_estimate=cost(0, 0),
        name="tap_query",
    )(*body_pieces, query_weights, from_chip, ring)
    from_far = [swap(piece, 1) for piece in onward]

    queries = pl.pallas_call(
        query_kernel,
        out_shape=tuple(jax.ShapeDtypeStruct((sum(parts) * TILE, width), bf16) for parts in CHUNKS),
        in_specs=vmem(7),
        out_specs=tuple(vmem(len(CHUNKS))),
        scratch_shapes=[pltpu.VMEM((2, FRAME, width), bf16)],
        compiler_params=params(),
        cost_estimate=cost(0, 0),
        name="query",
    )(
        tap_queries,
        rest_across,
        from_core,
        from_chip,
        from_far[0],
        from_far[1],
        query_weights,
    )

    count = (2 * REACH + 1) * block_rows
    heads = width // HDIM
    sends = [tiles for parts in CHUNKS for tiles in parts]
    starts = [sum(sends[:i]) for i in range(len(sends))]
    first = half // width
    pieces = []
    came = []
    marks = []
    result = None

    def attend(i, parts, query):
        waited = [pieces[-1][0]] if pieces else []
        waited += marks[:1] if i == 3 else []
        waited += came[i - 2 : i - 1] if i >= 2 else []
        outs = pl.pallas_call(
            functools.partial(attend_kernel, len(parts)),
            out_shape=tuple(jax.ShapeDtypeStruct((tiles * TILE, width), bf16) for tiles in parts),
            in_specs=vmem(4) + [anywhere] * len(waited),
            out_specs=tuple(vmem(len(parts))),
            scratch_shapes=[
                pltpu.VMEM((2 * edge + ring.shape[0], 2 * width), bf16),
                pltpu.VMEM((heads, count, width), bf16),
                pltpu.VMEM((heads, count, width), bf16),
            ],
            compiler_params=params(30),
            cost_estimate=cost(0, 0),
            name=f"attend{i}",
        )(query, before, ring, after, *waited)
        for out in outs:
            came.append(swap(out, 2))
            pieces.append((out, swap(out, 1), came[-1]))

    def finish(i, result):
        own, beside, across = pieces[i]
        extra = () if result is None else (result,)
        n = min(i + 2, 3)
        if i < n:
            onward, later = lax.optimization_barrier((across, pieces[n][0]))
            pieces[n] = (later, *pieces[n][1:])
        else:
            onward, later = lax.optimization_barrier((across, marks[i - 1 if i == 4 else 1]))
            extra = (*extra, later)
        start, tiles = starts[i], sends[i]
        result, mark = pl.pallas_call(
            out_kernel,
            grid=(tiles,),
            out_shape=(jax.ShapeDtypeStruct((rows, width), bf16), jax.ShapeDtypeStruct((8, 128), jnp.float32)),
            in_specs=[pl.BlockSpec((TILE, width), lambda s: (s, 0))] * 4
            + [pl.BlockSpec((width, width), lambda s, at=at: (at, 0)) for at in (0, first, first, 1)]
            + [pl.BlockSpec((TILE, width), lambda s: (start + s, 0))]
            + [anywhere] * len(extra),
            out_specs=(
                pl.BlockSpec((TILE, width), lambda s: (start + s, 0)),
                pl.BlockSpec((8, 128), lambda s: (0, 0)),
            ),
            input_output_aliases={9: 0} if extra else {},
            compiler_params=params(),
            cost_estimate=cost(0, 0),
            name=f"out{i}",
        )(own, beside, across, swap(onward, 1), w_own, from_core, from_chip, from_far[2], tokens, *extra)
        marks.append(mark)
        return result

    for i in range(3):
        attend(i, CHUNKS[i], queries[i])
    result = finish(0, result)
    attend(3, CHUNKS[3], queries[3])
    for i in range(1, len(sends)):
        result = finish(i, result)
    return result


def solution(mesh):
    return jax.shard_map(
        per_device,
        mesh=mesh,
        in_specs=(
            P("tm", "chan"),
            P(None, "chan"),
            P(None, "chan"),
            P(None, "chan"),
            P("chan", None),
            P(),
        ),
        out_specs=P("tm", "chan"),
        check_vma=False,
    )
```

```python
import functools
import math

import jax
import jax.numpy as jnp
import ml_dtypes
import numpy as np
from jax import lax
from jax.experimental import pallas as pl
from jax.experimental.pallas import tpu as pltpu
from jax.sharding import PartitionSpec as P

D = 1024
HDIM = 64
HH = 16
WW = 16
FRAME = HH * WW
POOL_ROWS = (HH // 4) * (WW // 4)
TAP_ROWS = FRAME // 2
RING = 8
REACH = 6
TILE = 256
CHUNKS = (1, 2, 2, 3)
EPSILON = 1e-06
MB = 1024 * 1024


def tap_order():
    wanted = []
    for second in range(3):
        for third in range(3):
            for row in range(HH // 4):
                for col in range(WW // 4):
                    i, j = 4 * row - 1 + second, 4 * col - 1 + third
                    wanted.append(i * WW + j if i >= 0 and j >= 0 else -1)
    used = sorted(set(t for t in wanted if t >= 0))
    order = np.array(used + [t for t in range(FRAME) if t not in set(used)])
    place = np.argsort(order)
    return order, np.array([place[t] if t >= 0 else -1 for t in wanted])


ORDER, TAP_PLACE = tap_order()
TAP_GATHER = (TAP_PLACE[:, None] == np.arange(TAP_ROWS)[None, :]).astype(ml_dtypes.bfloat16)


def place_of(token):
    i, j = token // WW, token % WW
    rows_before, cols_before = i - (i + 1) // 4, j - (j + 1) // 4
    row_used = (i % 4 != 2) & (i != HH - 1)
    col_used = (j % 4 != 2) & (j != WW - 1)
    side = HH - 1 - HH // 4
    used_before = rows_before * side + jnp.where(row_used, cols_before, 0)
    return jnp.where(row_used & col_used, used_before, side * side + token - used_before)


def move_matrix(back):
    token = lax.broadcasted_iota(jnp.int32, (FRAME, 1) if back else (1, FRAME), 0 if back else 1)
    place = lax.broadcasted_iota(jnp.int32, (FRAME, FRAME), 1 if back else 0)
    return jnp.where(place_of(token) == place, 1.0, 0.0).astype(jnp.bfloat16)


def vmem(count):
    return [pl.BlockSpec(memory_space=pltpu.VMEM)] * count


def params(limit=20):
    return pltpu.CompilerParams(vmem_limit_bytes=limit * MB)


def cost(flops, moved, exps=0):
    return pl.CostEstimate(flops=int(flops), bytes_accessed=int(moved), transcendentals=int(exps))


def dot(a, b):
    return jnp.dot(a, b, preferred_element_type=jnp.float32)


def arrange_kernel(
    tokens_hbm, w_out_hbm, taps_ref, last_ref, across_ref, beside_ref, own_ref, tokens_ref, w_out_ref, frame_sems, w_sem
):
    me = lax.axis_index("chan")
    frames = tokens_ref.shape[0] // FRAME
    count = frames * TAP_ROWS
    width = w_out_ref.shape[0]
    order = [frames - 1] + list(range(frames - 1))

    def frame_copy(f):
        rows = pl.ds(f * FRAME, FRAME)
        return pltpu.make_async_copy(tokens_hbm.at[rows, :], tokens_ref.at[rows, :], frame_sems.at[f])

    for f in order:
        frame_copy(f).start()
    w_copy = pltpu.make_async_copy(w_out_hbm, w_out_ref, w_sem)
    w_copy.start()
    gather = move_matrix(False)
    for f in order:
        frame_copy(f).wait()
        moved = dot(gather, tokens_ref[f * FRAME : (f + 1) * FRAME, :]).astype(jnp.bfloat16)
        taps_ref[f * TAP_ROWS : (f + 1) * TAP_ROWS, :] = moved[:TAP_ROWS]
        if f == frames - 1:
            last_ref[...] = moved[:TAP_ROWS]
        across_ref[f * TAP_ROWS : (f + 1) * TAP_ROWS, :] = moved[TAP_ROWS:]
        beside_ref[f * TAP_ROWS : (f + 1) * TAP_ROWS, :] = moved[TAP_ROWS:]
    w_copy.wait()

    def columns(k):
        return w_out_ref[:, pl.ds(pl.multiple_of((me ^ k) * width, width), width)]

    own_ref[...] = columns(0)
    beside_ref[count:, :] = columns(1)
    across_ref[count : count + width, :] = columns(2)
    across_ref[count + width :, :] = columns(3)


def pack_kernel(wk_hbm, wv_hbm, wq_hbm, pool_ref, key_value_ref, query_ref, taps_ref, sems):
    me = lax.axis_index("chan")
    width = query_ref.shape[1]
    copies = []
    for k in range(4):
        source = pl.ds(pl.multiple_of((me ^ k) * width, width), width)
        target = pl.ds(k * width, width)
        copies += [
            pltpu.make_async_copy(
                wk_hbm.at[source, :], key_value_ref.at[target, pl.ds(0, width)], sems.at[3 * k]
            ),
            pltpu.make_async_copy(
                wv_hbm.at[source, :], key_value_ref.at[target, pl.ds(width, width)], sems.at[3 * k + 1]
            ),
            pltpu.make_async_copy(wq_hbm.at[source, :], query_ref.at[target, :], sems.at[3 * k + 2]),
        ]
    for copy in copies:
        copy.start()
    heads = width // HDIM
    taps_ref[...] = jnp.concatenate([pool_ref[0]] * heads + [pool_ref[1]] * heads, axis=1)
    for copy in copies:
        copy.wait()


def project(pieces, start, count, weights):
    rows = jnp.concatenate([piece[start : start + count, :] for piece in pieces], axis=1)
    return dot(rows, weights).astype(jnp.bfloat16)


def weigh(slabs, taps, first):
    total = None
    for q in range(9):
        term = slabs[q * POOL_ROWS : (q + 1) * POOL_ROWS] * taps[9 * first + q : 9 * first + q + 1, :]
        total = term if total is None else total + term
    return total


def group_mean(rows, averaging):
    high = rows.astype(jnp.bfloat16)
    rest = rows - high.astype(jnp.float32)
    middle = rest.astype(jnp.bfloat16)
    low = (rest - middle.astype(jnp.float32)).astype(jnp.bfloat16)
    return dot(high, averaging) + dot(middle, averaging) + dot(low, averaging)


def pool_kernel_body(a0, a1, a2, a3, l0, l1, l2, l3, weights_ref, taps_ref, spread_ref, out_ref):
    width = weights_ref.shape[1] // 2
    lane = lax.broadcasted_iota(jnp.int32, (width, width), 1) // HDIM
    row = lax.broadcasted_iota(jnp.int32, (width, width), 0) // HDIM
    averaging = jnp.where(lane == row, 1.0 / HDIM, 0.0).astype(jnp.bfloat16)
    frames = a0.shape[0] // TAP_ROWS
    pooled_frames = frames // 2
    weights = weights_ref[...]
    taps = taps_ref[...]
    spread = spread_ref[...]
    sums = [None] * pooled_frames
    sums[0] = weigh(dot(spread, project((l0, l1, l2, l3), 0, TAP_ROWS, weights)), taps, 0)
    for f in range(frames):
        slabs = dot(spread, project((a0, a1, a2, a3), f * TAP_ROWS, TAP_ROWS, weights))
        t = f // 2
        part = weigh(slabs, taps, 1 + f % 2)
        sums[t] = part if sums[t] is None else sums[t] + part
        if f % 2 == 1 and t + 1 < pooled_frames:
            sums[t + 1] = weigh(slabs, taps, 0)
    pooled = jnp.concatenate(sums, axis=0)
    for side in range(2):
        lanes = slice(side * width, (side + 1) * width)
        center = pooled[:, lanes] - group_mean(pooled[:, lanes], averaging)
        spread_rows = group_mean(center * center, averaging)
        normal = (center * lax.rsqrt(spread_rows + EPSILON)).astype(jnp.bfloat16)
        for copy in range(out_ref.shape[0]):
            out_ref[copy, :, lanes] = normal


def tap_query_kernel(a0, a1, a2, a3, wq_ref, came_ref, after_ref, q_ref, *parts):
    del after_ref
    step = 2 * FRAME
    for start in range(0, q_ref.shape[0], step):
        q_ref[start : start + step, :] = project((a0, a1, a2, a3), start, step, wq_ref[...])
    at = 0
    for part in parts:
        part[...] = came_ref[at : at + part.shape[0], :]
        at += part.shape[0]


def query_kernel(q_ref, b0, b1, b2, c0, c1, wq_ref, *rest):
    outs, both = rest[:-1], rest[-1]
    frames = q_ref.shape[0] // TAP_ROWS
    back = move_matrix(True)
    places = [(ref, start) for ref in outs for start in range(0, ref.shape[0], FRAME)]
    far = c0.shape[0]
    for f in range(frames):
        at = f * TAP_ROWS
        both[f % 2, :TAP_ROWS, :] = q_ref[at : at + TAP_ROWS, :]
        c = c0 if at < far else c1
        pieces = [piece[at : at + TAP_ROWS, :] for piece in (b0, b1, b2)] + [c[at % far : at % far + TAP_ROWS, :]]
        others = dot(jnp.concatenate(pieces, axis=1), wq_ref[...])
        both[f % 2, TAP_ROWS:, :] = others.astype(jnp.bfloat16)
        ref, start = places[f]
        ref[start : start + FRAME, :] = dot(back, both[f % 2]).astype(jnp.bfloat16)


def ends_kernel(ring_ref, head_ref, tail_ref):
    edge = head_ref.shape[0]
    head_ref[...] = ring_ref[:edge, :]
    tail_ref[...] = ring_ref[ring_ref.shape[0] - edge :, :]


def attend_kernel(q_ref, before_ref, here_ref, after_ref, *rest):
    out_ref, window, keys, values = rest[-4:]
    width = q_ref.shape[1]
    heads = width // HDIM
    block = here_ref.shape[0] // RING
    count = keys.shape[1]
    z = lax.rem(lax.axis_index("tm"), RING)

    n = before_ref.shape[0]
    m = here_ref.shape[0]
    window[:n, :] = before_ref[...]
    window[n : n + m, :] = here_ref[...]
    window[n + m :, :] = after_ref[...]
    rows = window[pl.ds(pl.multiple_of(z * block, block), count), :]
    head = lax.broadcasted_iota(jnp.int32, (count, width), 1) // HDIM
    k = rows[:, :width].astype(jnp.float32) * (1.0 / math.sqrt(HDIM))
    v = rows[:, width:].astype(jnp.float32)
    for h in range(heads):
        keys[h] = jnp.where(head == h, k, 0.0).astype(jnp.bfloat16)
        values[h] = jnp.where(head == h, v, 0.0).astype(jnp.bfloat16)

    q = q_ref[...]
    total = q.astype(jnp.float32)
    for h in range(heads):
        scores = lax.dot_general(q, keys[h], (((1,), (1,)), ((), ())), preferred_element_type=jnp.float32)
        top = jnp.max(scores, axis=-1, keepdims=True)
        weighted = jnp.exp(scores - top)
        summed = jnp.sum(weighted, axis=-1, keepdims=True)
        total = total + dot(weighted.astype(jnp.bfloat16), values[h]) * (1.0 / summed)
    out_ref[...] = total.astype(jnp.bfloat16)


def out_kernel(a0, a1, a2, a3, w0, w1, w2, w3, tokens_ref, *rest):
    out_ref, done_ref = rest[-2:]
    done_ref[...] = jnp.zeros_like(done_ref)
    total = tokens_ref[...].astype(jnp.float32)
    acc = dot(a0[...], w0[...])
    for a, w in ((a1, w1), (a2, w2), (a3, w3)):
        acc = acc + dot(a[...], w[...])
    out_ref[...] = (total + acc).astype(jnp.bfloat16)


def swap(array, k):
    return lax.ppermute(array, "chan", [(i, i ^ k) for i in range(4)])


def per_device(tokens, w_query, w_key, w_value, w_out, pool_kernel):
    rows, width = tokens.shape
    frames = rows // FRAME
    devices = lax.axis_size("tm")
    bf16 = jnp.bfloat16
    tap_gather = jnp.asarray(TAP_GATHER)
    anywhere = pl.BlockSpec(memory_space=pl.ANY)

    hbm = pl.BlockSpec(memory_space=pltpu.HBM)
    half = frames * TAP_ROWS
    body, last, rest_across, rest_beside, w_own = pl.pallas_call(
        arrange_kernel,
        out_shape=(
            jax.ShapeDtypeStruct((half, width), bf16),
            jax.ShapeDtypeStruct((TAP_ROWS, width), bf16),
            jax.ShapeDtypeStruct((half + 2 * width, width), bf16),
            jax.ShapeDtypeStruct((half + width, width), bf16),
            jax.ShapeDtypeStruct((width, width), bf16),
        ),
        in_specs=[hbm] * 2,
        out_specs=tuple(vmem(5)),
        scratch_shapes=[
            pltpu.VMEM((rows, width), bf16),
            pltpu.VMEM((width, D), bf16),
            pltpu.SemaphoreType.DMA((frames,)),
            pltpu.SemaphoreType.DMA,
        ],
        compiler_params=params(60),
        cost_estimate=cost(2 * rows * FRAME * width, 4 * rows * width),
        name="arrange",
    )(tokens, w_out)
    key_value_weights, query_weights, taps = pl.pallas_call(
        pack_kernel,
        out_shape=(
            jax.ShapeDtypeStruct((D, 2 * width), bf16),
            jax.ShapeDtypeStruct((D, width), bf16),
            jax.ShapeDtypeStruct((pool_kernel.shape[1], 2 * width), jnp.float32),
        ),
        in_specs=[hbm] * 3 + vmem(1),
        out_specs=tuple(vmem(3)),
        scratch_shapes=[pltpu.SemaphoreType.DMA((12,))],
        compiler_params=params(8),
        cost_estimate=cost(0, 12 * D * width),
        name="pack",
    )(w_key, w_value, w_query, pool_kernel)
    last = lax.ppermute(last, "tm", [(i, (i + 1) % devices) for i in range(devices)])

    last, key_value_weights = lax.optimization_barrier((last, key_value_weights))
    last_across = swap(last, 2)
    body_across, last_across = lax.optimization_barrier((swap(body, 2), last_across))
    body_pieces = (body, swap(body, 1), body_across, swap(body_across, 1))
    last_pieces = (last, swap(last, 1), last_across, swap(last_across, 1))
    rest_later, last_came = lax.optimization_barrier((rest_across, last_pieces[2]))
    last_pieces = (*last_pieces[:2], last_came, last_pieces[3])
    from_chip = swap(rest_later, 2)
    from_core = swap(rest_beside, 1)

    block = pl.pallas_call(
        pool_kernel_body,
        out_shape=jax.ShapeDtypeStruct((RING, frames // 2 * POOL_ROWS, 2 * width), bf16),
        in_specs=vmem(11),
        out_specs=vmem(1)[0],
        compiler_params=params(),
        cost_estimate=cost(2 * frames * TAP_ROWS * D * 2 * width, 8 * rows * width),
        name="pool",
    )(*body_pieces, *last_pieces, key_value_weights, taps, tap_gather)

    block_rows = block.shape[1]
    rings = [[RING * r + z for z in range(RING)] for r in range(devices // RING)]
    ring = lax.all_to_all(block, "tm", 0, 0, axis_index_groups=rings).reshape(RING * block_rows, 2 * width)
    edge = (RING - 2) * block_rows
    head, tail = pl.pallas_call(
        ends_kernel,
        out_shape=(jax.ShapeDtypeStruct((edge, 2 * width), bf16), jax.ShapeDtypeStruct((edge, 2 * width), bf16)),
        in_specs=vmem(1),
        out_specs=tuple(vmem(2)),
        compiler_params=params(),
        cost_estimate=cost(0, 8 * edge * width),
        name="ends",
    )(ring)
    before = lax.ppermute(tail, "tm", [(i, (i + RING) % devices) for i in range(devices)])
    after = lax.ppermute(head, "tm", [((i + RING) % devices, i) for i in range(devices)])
    tap_queries, *onward = pl.pallas_call(
        tap_query_kernel,
        out_shape=tuple(jax.ShapeDtypeStruct((n, width), bf16) for n in (half, half // 2, half // 2, 2 * width)),
        in_specs=vmem(6) + [anywhere],
        out_specs=tuple(vmem(4)),
        compiler_params=params(),
        cost_estimate=cost(0, 0),
        name="tap_query",
    )(*body_pieces, query_weights, from_chip, ring)
    from_far = [swap(piece, 1) for piece in onward]

    queries = pl.pallas_call(
        query_kernel,
        out_shape=tuple(jax.ShapeDtypeStruct((n * TILE, width), bf16) for n in CHUNKS),
        in_specs=vmem(7),
        out_specs=tuple(vmem(len(CHUNKS))),
        scratch_shapes=[pltpu.VMEM((2, FRAME, width), bf16)],
        compiler_params=params(),
        cost_estimate=cost(0, 0),
        name="query",
    )(
        tap_queries,
        rest_across,
        from_core,
        from_chip,
        from_far[0],
        from_far[1],
        query_weights,
    )

    count = (2 * REACH + 1) * block_rows
    heads = width // HDIM
    starts = [sum(CHUNKS[:i]) for i in range(len(CHUNKS))]
    first = half // width
    attended = []
    came = []
    marks = []
    result = None

    def attend(i):
        chunk = CHUNKS[i] * TILE
        waited = attended[-1:] + (marks[-1:] if i == 3 else []) + (came[i - 2 : i - 1] if i >= 2 else [])
        out = pl.pallas_call(
            attend_kernel,
            out_shape=jax.ShapeDtypeStruct((chunk, width), bf16),
            in_specs=vmem(4) + [anywhere] * len(waited),
            out_specs=vmem(1)[0],
            scratch_shapes=[
                pltpu.VMEM((2 * edge + ring.shape[0], 2 * width), bf16),
                pltpu.VMEM((heads, count, width), bf16),
                pltpu.VMEM((heads, count, width), bf16),
            ],
            compiler_params=params(30),
            cost_estimate=cost(0, 0),
            name=f"attend{i}",
        )(queries[i], before, ring, after, *waited)
        attended.append(out)
        came.append(swap(out, 2))
        return out, swap(out, 1), came[-1]

    def finish(i, pieces, result):
        own, beside, across = pieces[i]
        extra = () if result is None else (result,)
        n = min(i + 2, len(CHUNKS) - 1)
        if i < n:
            onward, later = lax.optimization_barrier((across, pieces[n][0]))
            pieces[n] = (later, *pieces[n][1:])
        else:
            onward, later = lax.optimization_barrier((across, marks[i - 1]))
            extra = (*extra, later)
        start, tiles = starts[i], CHUNKS[i]
        result, mark = pl.pallas_call(
            out_kernel,
            grid=(tiles,),
            out_shape=(jax.ShapeDtypeStruct((rows, width), bf16), jax.ShapeDtypeStruct((8, 128), jnp.float32)),
            in_specs=[pl.BlockSpec((TILE, width), lambda s: (s, 0))] * 4
            + [pl.BlockSpec((width, width), lambda s, at=at: (at, 0)) for at in (0, first, first, 1)]
            + [pl.BlockSpec((TILE, width), lambda s: (start + s, 0))]
            + [anywhere] * len(extra),
            out_specs=(
                pl.BlockSpec((TILE, width), lambda s: (start + s, 0)),
                pl.BlockSpec((8, 128), lambda s: (0, 0)),
            ),
            input_output_aliases={9: 0} if extra else {},
            compiler_params=params(),
            cost_estimate=cost(0, 0),
            name=f"out{i}",
        )(own, beside, across, swap(onward, 1), w_own, from_core, from_chip, from_far[2], tokens, *extra)
        marks.append(mark)
        return result

    pieces = [attend(i) for i in range(3)]
    for i in range(len(CHUNKS)):
        result = finish(i, pieces, result)
        if i + 3 < len(CHUNKS):
            pieces.append(attend(i + 3))
    return result


def solution(mesh):
    return jax.shard_map(
        per_device,
        mesh=mesh,
        in_specs=(
            P("tm", "chan"),
            P(None, "chan"),
            P(None, "chan"),
            P(None, "chan"),
            P("chan", None),
            P(),
        ),
        out_specs=P("tm", "chan"),
        check_vma=False,
    )
```

```python
import functools
import math

import jax
import jax.numpy as jnp
import ml_dtypes
import numpy as np
from jax import lax
from jax.experimental import pallas as pl
from jax.experimental.pallas import tpu as pltpu
from jax.sharding import PartitionSpec as P

D = 1024
HDIM = 64
HH = 16
WW = 16
FRAME = HH * WW
POOL_ROWS = (HH // 4) * (WW // 4)
TAP_ROWS = FRAME // 2
RING = 8
REACH = 6
TILE = 256
CHUNKS = ((1,), (2,), (2,), (1, 2))
EPSILON = 1e-06
MB = 1024 * 1024


def tap_order():
    wanted = []
    for second in range(3):
        for third in range(3):
            for row in range(HH // 4):
                for col in range(WW // 4):
                    i, j = 4 * row - 1 + second, 4 * col - 1 + third
                    wanted.append(i * WW + j if i >= 0 and j >= 0 else -1)
    used = sorted(set(t for t in wanted if t >= 0))
    order = np.array(used + [t for t in range(FRAME) if t not in set(used)])
    place = np.argsort(order)
    return order, np.array([place[t] if t >= 0 else -1 for t in wanted])


ORDER, TAP_PLACE = tap_order()
TAP_GATHER = (TAP_PLACE[:, None] == np.arange(TAP_ROWS)[None, :]).astype(ml_dtypes.bfloat16)


def place_of(token):
    i, j = token // WW, token % WW
    rows_before, cols_before = i - (i + 1) // 4, j - (j + 1) // 4
    row_used = (i % 4 != 2) & (i != HH - 1)
    col_used = (j % 4 != 2) & (j != WW - 1)
    side = HH - 1 - HH // 4
    used_before = rows_before * side + jnp.where(row_used, cols_before, 0)
    return jnp.where(row_used & col_used, used_before, side * side + token - used_before)


def move_matrix(back):
    token = lax.broadcasted_iota(jnp.int32, (FRAME, 1) if back else (1, FRAME), 0 if back else 1)
    place = lax.broadcasted_iota(jnp.int32, (FRAME, FRAME), 1 if back else 0)
    return jnp.where(place_of(token) == place, 1.0, 0.0).astype(jnp.bfloat16)


def vmem(count):
    return [pl.BlockSpec(memory_space=pltpu.VMEM)] * count


def params(limit=20):
    return pltpu.CompilerParams(vmem_limit_bytes=limit * MB)


def cost(flops, moved, exps=0):
    return pl.CostEstimate(flops=int(flops), bytes_accessed=int(moved), transcendentals=int(exps))


def dot(a, b):
    return jnp.dot(a, b, preferred_element_type=jnp.float32)


def arrange_kernel(
    tokens_hbm, w_out_hbm, taps_ref, last_ref, across_ref, beside_ref, own_ref, tokens_ref, w_out_ref, frame_sems, w_sem
):
    me = lax.axis_index("chan")
    frames = tokens_ref.shape[0] // FRAME
    count = frames * TAP_ROWS
    width = w_out_ref.shape[0]
    order = [frames - 1] + list(range(frames - 1))

    def frame_copy(f):
        rows = pl.ds(f * FRAME, FRAME)
        return pltpu.make_async_copy(tokens_hbm.at[rows, :], tokens_ref.at[rows, :], frame_sems.at[f])

    for f in order:
        frame_copy(f).start()
    w_copy = pltpu.make_async_copy(w_out_hbm, w_out_ref, w_sem)
    w_copy.start()
    gather = move_matrix(False)
    for f in order:
        frame_copy(f).wait()
        moved = dot(gather, tokens_ref[f * FRAME : (f + 1) * FRAME, :]).astype(jnp.bfloat16)
        taps_ref[f * TAP_ROWS : (f + 1) * TAP_ROWS, :] = moved[:TAP_ROWS]
        if f == frames - 1:
            last_ref[...] = moved[:TAP_ROWS]
        across_ref[f * TAP_ROWS : (f + 1) * TAP_ROWS, :] = moved[TAP_ROWS:]
        beside_ref[f * TAP_ROWS : (f + 1) * TAP_ROWS, :] = moved[TAP_ROWS:]
    w_copy.wait()

    def columns(k):
        return w_out_ref[:, pl.ds(pl.multiple_of((me ^ k) * width, width), width)]

    own_ref[...] = columns(0)
    beside_ref[count:, :] = columns(1)
    across_ref[count : count + width, :] = columns(2)
    across_ref[count + width :, :] = columns(3)


def pack_kernel(wk_hbm, wv_hbm, wq_hbm, pool_ref, key_value_ref, query_ref, taps_ref, sems):
    me = lax.axis_index("chan")
    width = query_ref.shape[1]
    copies = []
    for k in range(4):
        source = pl.ds(pl.multiple_of((me ^ k) * width, width), width)
        target = pl.ds(k * width, width)
        copies += [
            pltpu.make_async_copy(
                wk_hbm.at[source, :], key_value_ref.at[target, pl.ds(0, width)], sems.at[3 * k]
            ),
            pltpu.make_async_copy(
                wv_hbm.at[source, :], key_value_ref.at[target, pl.ds(width, width)], sems.at[3 * k + 1]
            ),
            pltpu.make_async_copy(wq_hbm.at[source, :], query_ref.at[target, :], sems.at[3 * k + 2]),
        ]
    for copy in copies:
        copy.start()
    heads = width // HDIM
    taps_ref[...] = jnp.concatenate([pool_ref[0]] * heads + [pool_ref[1]] * heads, axis=1)
    for copy in copies:
        copy.wait()


def project(pieces, start, count, weights):
    rows = jnp.concatenate([piece[start : start + count, :] for piece in pieces], axis=1)
    return dot(rows, weights).astype(jnp.bfloat16)


def weigh(slabs, taps, first):
    total = None
    for q in range(9):
        term = slabs[q * POOL_ROWS : (q + 1) * POOL_ROWS] * taps[9 * first + q : 9 * first + q + 1, :]
        total = term if total is None else total + term
    return total


def group_mean(rows, averaging):
    high = rows.astype(jnp.bfloat16)
    rest = rows - high.astype(jnp.float32)
    middle = rest.astype(jnp.bfloat16)
    low = (rest - middle.astype(jnp.float32)).astype(jnp.bfloat16)
    return dot(high, averaging) + dot(middle, averaging) + dot(low, averaging)


def pool_kernel_body(a0, a1, a2, a3, l0, l1, l2, l3, weights_ref, taps_ref, spread_ref, out_ref):
    width = weights_ref.shape[1] // 2
    lane = lax.broadcasted_iota(jnp.int32, (width, width), 1) // HDIM
    row = lax.broadcasted_iota(jnp.int32, (width, width), 0) // HDIM
    averaging = jnp.where(lane == row, 1.0 / HDIM, 0.0).astype(jnp.bfloat16)
    frames = a0.shape[0] // TAP_ROWS
    pooled_frames = frames // 2
    weights = weights_ref[...]
    taps = taps_ref[...]
    spread = spread_ref[...]
    sums = [None] * pooled_frames
    sums[0] = weigh(dot(spread, project((l0, l1, l2, l3), 0, TAP_ROWS, weights)), taps, 0)
    for f in range(frames):
        slabs = dot(spread, project((a0, a1, a2, a3), f * TAP_ROWS, TAP_ROWS, weights))
        t = f // 2
        part = weigh(slabs, taps, 1 + f % 2)
        sums[t] = part if sums[t] is None else sums[t] + part
        if f % 2 == 1 and t + 1 < pooled_frames:
            sums[t + 1] = weigh(slabs, taps, 0)
    pooled = jnp.concatenate(sums, axis=0)
    for side in range(2):
        lanes = slice(side * width, (side + 1) * width)
        center = pooled[:, lanes] - group_mean(pooled[:, lanes], averaging)
        spread_rows = group_mean(center * center, averaging)
        normal = (center * lax.rsqrt(spread_rows + EPSILON)).astype(jnp.bfloat16)
        for copy in range(out_ref.shape[0]):
            out_ref[copy, :, lanes] = normal


def tap_query_kernel(a0, a1, a2, a3, wq_ref, came_ref, after_ref, q_ref, *parts):
    del after_ref
    step = 2 * FRAME
    for start in range(0, q_ref.shape[0], step):
        q_ref[start : start + step, :] = project((a0, a1, a2, a3), start, step, wq_ref[...])
    at = 0
    for part in parts:
        part[...] = came_ref[at : at + part.shape[0], :]
        at += part.shape[0]


def query_kernel(q_ref, b0, b1, b2, c0, c1, wq_ref, *rest):
    outs, both = rest[:-1], rest[-1]
    frames = q_ref.shape[0] // TAP_ROWS
    back = move_matrix(True)
    places = [(ref, start) for ref in outs for start in range(0, ref.shape[0], FRAME)]
    far = c0.shape[0]
    for f in range(frames):
        at = f * TAP_ROWS
        both[f % 2, :TAP_ROWS, :] = q_ref[at : at + TAP_ROWS, :]
        c = c0 if at < far else c1
        pieces = [piece[at : at + TAP_ROWS, :] for piece in (b0, b1, b2)] + [c[at % far : at % far + TAP_ROWS, :]]
        others = dot(jnp.concatenate(pieces, axis=1), wq_ref[...])
        both[f % 2, TAP_ROWS:, :] = others.astype(jnp.bfloat16)
        ref, start = places[f]
        ref[start : start + FRAME, :] = dot(back, both[f % 2]).astype(jnp.bfloat16)


def ends_kernel(ring_ref, head_ref, tail_ref):
    edge = head_ref.shape[0]
    head_ref[...] = ring_ref[:edge, :]
    tail_ref[...] = ring_ref[ring_ref.shape[0] - edge :, :]


def attend_kernel(parts, q_ref, before_ref, here_ref, after_ref, *rest):
    outs, (window, keys, values) = rest[-3 - parts : -3], rest[-3:]
    width = q_ref.shape[1]
    heads = width // HDIM
    block = here_ref.shape[0] // RING
    count = keys.shape[1]
    z = lax.rem(lax.axis_index("tm"), RING)

    n = before_ref.shape[0]
    m = here_ref.shape[0]
    window[:n, :] = before_ref[...]
    window[n : n + m, :] = here_ref[...]
    window[n + m :, :] = after_ref[...]
    rows = window[pl.ds(pl.multiple_of(z * block, block), count), :]
    head = lax.broadcasted_iota(jnp.int32, (count, width), 1) // HDIM
    k = rows[:, :width].astype(jnp.float32) * (1.0 / math.sqrt(HDIM))
    v = rows[:, width:].astype(jnp.float32)
    for h in range(heads):
        keys[h] = jnp.where(head == h, k, 0.0).astype(jnp.bfloat16)
        values[h] = jnp.where(head == h, v, 0.0).astype(jnp.bfloat16)

    q = q_ref[...]
    total = q.astype(jnp.float32)
    for h in range(heads):
        scores = lax.dot_general(q, keys[h], (((1,), (1,)), ((), ())), preferred_element_type=jnp.float32)
        top = jnp.max(scores, axis=-1, keepdims=True)
        weighted = jnp.exp(scores - top)
        summed = jnp.sum(weighted, axis=-1, keepdims=True)
        total = total + dot(weighted.astype(jnp.bfloat16), values[h]) * (1.0 / summed)
    at = 0
    for ref in outs:
        ref[...] = total[at : at + ref.shape[0]].astype(jnp.bfloat16)
        at += ref.shape[0]


def out_kernel(a0, a1, a2, a3, w0, w1, w2, w3, tokens_ref, *rest):
    out_ref, done_ref = rest[-2:]
    done_ref[...] = jnp.zeros_like(done_ref)
    total = tokens_ref[...].astype(jnp.float32)
    acc = dot(a0[...], w0[...])
    for a, w in ((a1, w1), (a2, w2), (a3, w3)):
        acc = acc + dot(a[...], w[...])
    out_ref[...] = (total + acc).astype(jnp.bfloat16)


def swap(array, k):
    return lax.ppermute(array, "chan", [(i, i ^ k) for i in range(4)])


def per_device(tokens, w_query, w_key, w_value, w_out, pool_kernel):
    rows, width = tokens.shape
    frames = rows // FRAME
    devices = lax.axis_size("tm")
    bf16 = jnp.bfloat16
    tap_gather = jnp.asarray(TAP_GATHER)
    anywhere = pl.BlockSpec(memory_space=pl.ANY)

    hbm = pl.BlockSpec(memory_space=pltpu.HBM)
    half = frames * TAP_ROWS
    body, last, rest_across, rest_beside, w_own = pl.pallas_call(
        arrange_kernel,
        out_shape=(
            jax.ShapeDtypeStruct((half, width), bf16),
            jax.ShapeDtypeStruct((TAP_ROWS, width), bf16),
            jax.ShapeDtypeStruct((half + 2 * width, width), bf16),
            jax.ShapeDtypeStruct((half + width, width), bf16),
            jax.ShapeDtypeStruct((width, width), bf16),
        ),
        in_specs=[hbm] * 2,
        out_specs=tuple(vmem(5)),
        scratch_shapes=[
            pltpu.VMEM((rows, width), bf16),
            pltpu.VMEM((width, D), bf16),
            pltpu.SemaphoreType.DMA((frames,)),
            pltpu.SemaphoreType.DMA,
        ],
        compiler_params=params(60),
        cost_estimate=cost(2 * rows * FRAME * width, 4 * rows * width),
        name="arrange",
    )(tokens, w_out)
    key_value_weights, query_weights, taps = pl.pallas_call(
        pack_kernel,
        out_shape=(
            jax.ShapeDtypeStruct((D, 2 * width), bf16),
            jax.ShapeDtypeStruct((D, width), bf16),
            jax.ShapeDtypeStruct((pool_kernel.shape[1], 2 * width), jnp.float32),
        ),
        in_specs=[hbm] * 3 + vmem(1),
        out_specs=tuple(vmem(3)),
        scratch_shapes=[pltpu.SemaphoreType.DMA((12,))],
        compiler_params=params(8),
        cost_estimate=cost(0, 12 * D * width),
        name="pack",
    )(w_key, w_value, w_query, pool_kernel)
    last = lax.ppermute(last, "tm", [(i, (i + 1) % devices) for i in range(devices)])

    last, key_value_weights = lax.optimization_barrier((last, key_value_weights))
    last_across = swap(last, 2)
    body_across, last_across = lax.optimization_barrier((swap(body, 2), last_across))
    body_pieces = (body, swap(body, 1), body_across, swap(body_across, 1))
    last_pieces = (last, swap(last, 1), last_across, swap(last_across, 1))
    rest_later, last_came = lax.optimization_barrier((rest_across, last_pieces[2]))
    last_pieces = (*last_pieces[:2], last_came, last_pieces[3])
    from_chip = swap(rest_later, 2)
    from_core = swap(rest_beside, 1)

    block = pl.pallas_call(
        pool_kernel_body,
        out_shape=jax.ShapeDtypeStruct((RING, frames // 2 * POOL_ROWS, 2 * width), bf16),
        in_specs=vmem(11),
        out_specs=vmem(1)[0],
        compiler_params=params(),
        cost_estimate=cost(2 * frames * TAP_ROWS * D * 2 * width, 8 * rows * width),
        name="pool",
    )(*body_pieces, *last_pieces, key_value_weights, taps, tap_gather)

    block_rows = block.shape[1]
    rings = [[RING * r + z for z in range(RING)] for r in range(devices // RING)]
    ring = lax.all_to_all(block, "tm", 0, 0, axis_index_groups=rings).reshape(RING * block_rows, 2 * width)
    edge = (RING - 2) * block_rows
    head, tail = pl.pallas_call(
        ends_kernel,
        out_shape=(jax.ShapeDtypeStruct((edge, 2 * width), bf16), jax.ShapeDtypeStruct((edge, 2 * width), bf16)),
        in_specs=vmem(1),
        out_specs=tuple(vmem(2)),
        compiler_params=params(),
        cost_estimate=cost(0, 8 * edge * width),
        name="ends",
    )(ring)
    before = lax.ppermute(tail, "tm", [(i, (i + RING) % devices) for i in range(devices)])
    after = lax.ppermute(head, "tm", [((i + RING) % devices, i) for i in range(devices)])
    tap_queries, *onward = pl.pallas_call(
        tap_query_kernel,
        out_shape=tuple(jax.ShapeDtypeStruct((n, width), bf16) for n in (half, half // 2, half // 2, 2 * width)),
        in_specs=vmem(6) + [anywhere],
        out_specs=tuple(vmem(4)),
        compiler_params=params(),
        cost_estimate=cost(0, 0),
        name="tap_query",
    )(*body_pieces, query_weights, from_chip, ring)
    from_far = [swap(piece, 1) for piece in onward]

    queries = pl.pallas_call(
        query_kernel,
        out_shape=tuple(jax.ShapeDtypeStruct((sum(parts) * TILE, width), bf16) for parts in CHUNKS),
        in_specs=vmem(7),
        out_specs=tuple(vmem(len(CHUNKS))),
        scratch_shapes=[pltpu.VMEM((2, FRAME, width), bf16)],
        compiler_params=params(),
        cost_estimate=cost(0, 0),
        name="query",
    )(
        tap_queries,
        rest_across,
        from_core,
        from_chip,
        from_far[0],
        from_far[1],
        query_weights,
    )

    count = (2 * REACH + 1) * block_rows
    heads = width // HDIM
    sends = [tiles for parts in CHUNKS for tiles in parts]
    starts = [sum(sends[:i]) for i in range(len(sends))]
    first = half // width
    pieces = []
    came = []
    marks = []
    result = None

    def attend(i, parts, query):
        waited = [pieces[-1][0]] if pieces else []
        waited += marks[:1] if i == 3 else []
        waited += came[i - 2 : i - 1] if i >= 2 else []
        outs = pl.pallas_call(
            functools.partial(attend_kernel, len(parts)),
            out_shape=tuple(jax.ShapeDtypeStruct((tiles * TILE, width), bf16) for tiles in parts),
            in_specs=vmem(4) + [anywhere] * len(waited),
            out_specs=tuple(vmem(len(parts))),
            scratch_shapes=[
                pltpu.VMEM((2 * edge + ring.shape[0], 2 * width), bf16),
                pltpu.VMEM((heads, count, width), bf16),
                pltpu.VMEM((heads, count, width), bf16),
            ],
            compiler_params=params(30),
            cost_estimate=cost(0, 0),
            name=f"attend{i}",
        )(query, before, ring, after, *waited)
        for out in outs:
            came.append(swap(out, 2))
            pieces.append((out, swap(out, 1), came[-1]))

    def finish(i, result):
        own, beside, across = pieces[i]
        extra = () if result is None else (result,)
        n = min(i + 2, 3)
        if i < n:
            onward, later = lax.optimization_barrier((across, pieces[n][0]))
            pieces[n] = (later, *pieces[n][1:])
        else:
            onward, later = lax.optimization_barrier((across, marks[i - 1 if i == 4 else 1]))
            extra = (*extra, later)
        start, tiles = starts[i], sends[i]
        result, mark = pl.pallas_call(
            out_kernel,
            grid=(tiles,),
            out_shape=(jax.ShapeDtypeStruct((rows, width), bf16), jax.ShapeDtypeStruct((8, 128), jnp.float32)),
            in_specs=[pl.BlockSpec((TILE, width), lambda s: (s, 0))] * 4
            + [pl.BlockSpec((width, width), lambda s, at=at: (at, 0)) for at in (0, first, first, 1)]
            + [pl.BlockSpec((TILE, width), lambda s: (start + s, 0))]
            + [anywhere] * len(extra),
            out_specs=(
                pl.BlockSpec((TILE, width), lambda s: (start + s, 0)),
                pl.BlockSpec((8, 128), lambda s: (0, 0)),
            ),
            input_output_aliases={9: 0} if extra else {},
            compiler_params=params(),
            cost_estimate=cost(0, 0),
            name=f"out{i}",
        )(own, beside, across, swap(onward, 1), w_own, from_core, from_chip, from_far[2], tokens, *extra)
        marks.append(mark)
        return result

    for i in range(3):
        attend(i, CHUNKS[i], queries[i])
    result = finish(0, result)
    attend(3, CHUNKS[3], queries[3])
    for i in range(1, len(sends)):
        result = finish(i, result)
    return result


def solution(mesh):
    return jax.shard_map(
        per_device,
        mesh=mesh,
        in_specs=(
            P("tm", "chan"),
            P(None, "chan"),
            P(None, "chan"),
            P(None, "chan"),
            P("chan", None),
            P(),
        ),
        out_specs=P("tm", "chan"),
        check_vma=False,
    )
```
